256 devices in a mesh: row: 32 (over z, y), col: 8 (over x, core).
Axes of the slice: x: 4, y: 4, z: 8, core: 2. Of those that a mesh axis runs over, the one named last changes fastest.
Arguments:
- head_deflections: float32 [256, 3, 2, 1024], P('row', None, None, 'col'), may hold values from -6 to 6
- diag_inverse: float32 [2, 1024, 1024], P(None, None, 'col'), may hold values from -1 to 2, as said below
- coupling: float32 [1024, 1024], P(None, 'col'), may hold values from -0.1875 to 0.1875
- panel_factor: float32 [32768, 2, 1024], P('row', None, 'col'), may hold values from -0.125 to 0.125
- trailing: float32 [256, 3, 32768], P('col', None, 'row'), may hold values from -6 to 6
Outputs:
- solved: float32 [256, 3, 2, 1024], P('row', None, None, 'col')
- rest: float32 [256, 3, 32768], P('col', None, 'row')
The draws below stay inside these ranges and needn't reach their ends.
Inputs may be any that keep to these rules, and one draw needn't show every extreme that they name: Each diag_inverse[p] is lower triangular with a positive diagonal.
All inputs are finite; a program needn't handle non-finite values.
Results may differ from the reference program's by a relative error of at most 0.00007.
Values sent between devices are 32-bit elements; how exact they have to be, the bound alone decides.
A program may use at most 64 MiB of HBM per device.

```python
import math
import jax
import jax.numpy as jnp
from jax import lax

NB = 1024
STEPS = 256
COMP = 3
TRAIL = 32768


def draw_diag_inverse(key, part):
    key_lower, key_diagonal = jax.random.split(key)
    rows = lax.broadcasted_iota(jnp.int32, (2, NB, NB), 1)
    cols = lax.broadcasted_iota(jnp.int32, (2, NB, NB), 2)
    lower = jax.random.normal(key_lower, (2, NB, NB), jnp.float32)
    lower = lower * (0.6 / math.sqrt(NB))
    diagonal = jnp.exp(jax.random.uniform(key_diagonal, (2, NB, NB), jnp.float32, math.log(0.5), math.log(1.5)))
    return jnp.where(rows > cols, lower, jnp.where(rows == cols, diagonal, 0.0))


def shard_levels(own_key, shape, shards, least, top_value):
    def one(axis_at, blocks):
        draws = jax.random.uniform(jax.random.fold_in(jax.random.fold_in(own_key, 6), axis_at), (blocks,), jnp.float32, least / len(shards), top_value / len(shards))
        return jnp.repeat(jnp.exp(draws), shape[axis_at] // blocks).reshape((-1,) + (1,) * (len(shape) - axis_at - 1))

    loudness = one(*shards[0])
    for cut in shards[1:]:
        loudness = loudness * one(*cut)
    return loudness


def gaussian(stream_key, extent, width, most, pieces=(), kind=jnp.bfloat16):
    drawn = jax.random.normal(stream_key, extent, jnp.float32) * width
    if len(pieces) > 0:
        drawn = shard_levels(stream_key, extent, pieces, -0.22, 0.18) * drawn
    return jnp.clip(drawn, min=-most, max=most).astype(kind)


def setup_inputs(seed: int = 0) -> dict:
    key_list = jax.random.split(jax.random.key(seed), 6)
    head_deflections = gaussian(key_list[0], (STEPS, COMP, 2, NB), 1.0, 6.0, ((0, 32), (3, 8)), jnp.float32)
    diag_inverse = draw_diag_inverse(jax.random.fold_in(key_list[5], 71), 0)
    coupling = gaussian(key_list[2], (NB, NB), NB ** -0.5, 0.1875, ((1, 8),), jnp.float32)
    panel_factor = gaussian(key_list[3], (TRAIL, 2, NB), (2 * NB) ** -0.5, 0.125, ((0, 32), (2, 8)), jnp.float32)
    trailing = gaussian(key_list[4], (STEPS, COMP, TRAIL), 1.0, 6.0, ((0, 8), (2, 32)), jnp.float32)
    return dict(head_deflections=head_deflections, diag_inverse=diag_inverse, coupling=coupling, panel_factor=panel_factor, trailing=trailing)


def reference(head_deflections, diag_inverse, coupling, panel_factor, trailing):
    highest = lax.Precision.HIGHEST
    first_solved = jnp.einsum("ij,skj->ski", diag_inverse[0], head_deflections[:, :, 0, :], precision=highest)
    carried = head_deflections[:, :, 1, :] - jnp.einsum("ij,skj->ski", coupling, first_solved, precision=highest)
    second_solved = jnp.einsum("ij,skj->ski", diag_inverse[1], carried, precision=highest)
    solved = jnp.stack([first_solved, second_solved], axis=2)
    first_update = jnp.einsum("rj,skj->skr", panel_factor[:, 0, :], first_solved, precision=highest)
    second_update = jnp.einsum("rj,skj->skr", panel_factor[:, 1, :], second_solved, precision=highest)
    rest = trailing - first_update - second_update
    return solved, rest
```

```python
import functools

import jax
import jax.numpy as jnp
from jax import lax
from jax.experimental import pallas as pl
from jax.experimental.pallas import tpu as pltpu
from jax.sharding import PartitionSpec as P

MESH = pl.DeviceIdType.MESH
F32 = jnp.float32
BF16 = jnp.bfloat16
NX, NY, NZ = 4, 4, 8
NC = 8
V = 24
W = 128
HALF = 512
LAG = 3
NT = (((1,), (1,)), ((), ()))


def split(value):
    high = value.astype(BF16)
    return high, (value - high.astype(F32)).astype(BF16)


def kernel(h_ref, d_ref, c_ref, f_ref, sol_ref, upd_ref,
           d_buf, c_buf, f_buf, ft_hi, ft_lo, part, got, S, acc, M, R, L,
           load_sem, fs, fr, a_ss, a_rs, y_ss, y_rs, z_ss, z_rs, p_ss, p_rs, e_ss, e_rs):
    row, col = lax.axis_index("row"), lax.axis_index("col")
    z, y = row // NY, row % NY
    x, k = col // 2, col % 2
    step_k = 1 - 2 * k
    mate = x * 2 + 1 - k
    next_z = (z + step_k + NZ) % NZ
    prev_z = (z - step_k + NZ) % NZ

    def place(zz, yy):
        return zz * NY + yy

    def remote(src, dst, ss, rs, to):
        return pltpu.make_async_remote_copy(
            src_ref=src, dst_ref=dst, send_sem=ss, recv_sem=rs, device_id=to, device_id_type=MESH)

    partner = (row, mate)
    ring_to = (place(next_z, y), col)

    barrier = pltpu.get_barrier_semaphore()
    friends = [(row, (col + o) % NC) for o in range(1, NC)]
    y_list = [(dy, dk) for dy in range(NY) for dk in range(2) if (dy, dk) != (0, 0)]
    y_dev = [(place(z, (y + dy) % NY), x * 2 + (k + dk) % 2) for dy, dk in y_list]
    friends += [dev for (dy, dk), dev in zip(y_list, y_dev) if dy]
    friends += [ring_to, (place(prev_z, y), col)]
    for dev in friends:
        pl.semaphore_signal(barrier, inc=1, device_id=dev, device_id_type=MESH)

    loads = [
        pltpu.make_async_copy(d_ref.at[0], d_buf.at[0], load_sem.at[0]),
        pltpu.make_async_copy(c_ref, c_buf, load_sem.at[1]),
        pltpu.make_async_copy(d_ref.at[1], d_buf.at[1], load_sem.at[2]),
    ]
    mine = pl.ds(pl.multiple_of(k * HALF, HALF), HALF)
    theirs = pl.ds(pl.multiple_of((1 - k) * HALF, HALF), HALF)
    for p in range(2):
        loads.append(pltpu.make_async_copy(f_ref.at[mine, p], f_buf.at[p, k], load_sem.at[3 + p]))
    for load in loads:
        load.start()

    def partial(stage, value, matrix):
        hi, lo = split(value)
        both = jnp.concatenate([hi, lo], axis=0)
        for b in range(NC):
            m_hi, m_lo = split(matrix[b * W:(b + 1) * W, :])
            one = lax.dot_general(both, m_hi, NT, preferred_element_type=F32)
            two = lax.dot_general(hi, m_lo, NT, preferred_element_type=F32)
            part[stage, b] = one[:V] + (one[V:] + two)

    def exchange(stage):
        copies = []
        for o in range(1, NC):
            to = (col + o) % NC
            copies.append(remote(part.at[stage, to], got.at[stage, o], a_ss.at[stage, o], a_rs.at[stage, o], (row, to)))
        for copy in copies:
            copy.start()
        return copies

    def collect(stage, copies):
        total = part[stage, col]
        for o in range(1, NC):
            copies[o - 1].wait_recv()
            total = total + got[stage, o]
        return total

    def share(p):
        copies = []
        for i, dev in enumerate(y_dev):
            here = S.at[p, z, k, y]
            copies.append(remote(here, here, y_ss.at[p, i], y_rs.at[p, i], dev))
        for copy in copies:
            copy.start()
        return copies

    def chunk(i):
        t = (i + 1) // 2
        sign = jnp.where(i % 2 == 1, -step_k, step_k)
        return (z + sign * t + NZ) % NZ

    def ring_send(p, t, c):
        return remote(S.at[p, c], S.at[p, c], z_ss.at[p, t], z_rs.at[p, t], ring_to)

    def ring_send_part(p, c):
        return remote(S.at[p, c, k], S.at[p, c, k], z_ss.at[p, 4], z_rs.at[p, 4], ring_to)

    def mate_send(p, t, c):
        return remote(S.at[p, c], S.at[p, c], p_ss.at[p, t], p_rs.at[p, t], partner)

    def mate_send_part(p, c):
        return remote(S.at[p, c, k], S.at[p, c, k], p_ss.at[p, 4], p_rs.at[p, 4], partner)

    def arrive(p, i):
        t = (i + 1) // 2
        c = chunk(i)

        @pl.when((i % 2 == 1) & (i < 7))
        def _():
            ring_send(p, t, c).wait_recv()

            @pl.when(i < 5)
            def _():
                ring_send(p, t + 1, c).start()

            @pl.when(i == 5)
            def _():
                ring_send_part(p, c).start()

            mate_send(p, t, c).start()

        @pl.when((i % 2 == 0) & (i > 0))
        def _():
            mate_send(p, t, c).wait_recv()

        @pl.when(i == 7)
        def _():
            ring_send_part(p, c).wait_recv()
            mate_send_part(p, c).start()
            mate_send_part(p, c).wait_recv()

    def update(p, c):
        s = jnp.concatenate([S[p, c, 0].reshape(4 * V, W), S[p, c, 1].reshape(4 * V, W)], axis=1)
        hi, lo = split(s)
        one = jnp.dot(jnp.concatenate([hi, lo], axis=0), ft_hi[p], preferred_element_type=F32)
        two = jnp.dot(hi, ft_lo[p], preferred_element_type=F32)
        return one[:4 * V] + (one[4 * V:] + two)

    loads[0].wait()
    partial(0, h_ref[0], d_buf.at[0])
    pl.semaphore_wait(barrier, len(friends))
    sent0 = exchange(0)
    f_sends = [remote(f_ref.at[theirs, p], f_buf.at[p, k], fs.at[p], fr.at[p], partner) for p in range(2)]
    for copy in f_sends:
        copy.start()
    loads[1].wait()
    loads[2].wait()
    first = collect(0, sent0)
    sol_ref[0] = first
    S[0, z, k, y] = first
    partial(1, first, c_buf)
    sent1 = exchange(1)
    shared0 = share(0)

    for p in range(2):
        loads[3 + p].wait()
        f_sends[p].wait_recv()
        for kk in range(2):
            hi, lo = split(f_buf[p, kk].T)
            ft_hi[p, kk * W:(kk + 1) * W, :] = hi
            ft_lo[p, kk * W:(kk + 1) * W, :] = lo

    carried = h_ref[1] - collect(1, sent1)
    partial(2, carried, d_buf.at[1])
    sent2 = exchange(2)
    for copy in shared0:
        copy.wait_recv()
    ring_send(0, 1, z).start()
    acc[z] = update(0, z)
    second = collect(2, sent2)
    sol_ref[1] = second
    S[1, z, k, y] = second
    shared1 = share(1)

    def first_loop(i, carry):
        arrive(0, i)
        c = chunk(i)
        acc[c] = update(0, c)
        return carry

    lax.fori_loop(1, 8, first_loop, 0)
    for copy in shared1:
        copy.wait_recv()
    ring_send(1, 1, z).start()

    up = (x + step_k + NX) % NX
    down = (x - step_k + NX) % NX

    def over(cc, c):
        return remote(acc.at[c], M.at[cc], e_ss.at[0, cc], e_rs.at[0, cc], (row, up * 2 + k))

    def merged(cc, c):
        return remote(acc.at[c], R.at[0, k], e_ss.at[1, cc], e_rs.at[1, k], (row, up * 2 + cc))

    def direct(cc, c):
        return remote(acc.at[c], R.at[1, k], e_ss.at[2, cc], e_rs.at[2, k], (row, down * 2 + cc))

    def local(c):
        return remote(acc.at[c], L.at[k], e_ss.at[3, 0], e_rs.at[3, 0], partner)

    def merge(i):
        c = chunk(i)
        cc = c % 2

        @pl.when(c // 2 == up)
        def _():
            over(cc, c).wait_recv()
            acc[c] = acc[c] + M[cc]
            merged(cc, c).start()

    def second_loop(i, carry):
        arrive(1, i)
        c = chunk(i)
        acc[c] = acc[c] + update(1, c)
        to, cc = c // 2, c % 2

        @pl.when((to != up) & (to != down) & (to != x))
        def _():
            over(cc, c).start()

        @pl.when(to == down)
        def _():
            direct(cc, c).start()

        @pl.when((to == x) & (cc != k))
        def _():
            local(c).start()

        @pl.when((to == x) & (cc == k))
        def _():
            L[k] = acc[c]

        @pl.when(i >= LAG)
        def _():
            merge(i - LAG)

        return carry

    lax.fori_loop(0, 8, second_loop, 0)

    def last_loop(i, carry):
        merge(i)
        return carry

    lax.fori_loop(8 - LAG, 8, last_loop, 0)

    local(z).wait_recv()
    for kk in range(2):
        remote(acc.at[0], R.at[1, kk], e_ss.at[2, 0], e_rs.at[2, kk], partner).wait_recv()
        remote(acc.at[0], R.at[0, kk], e_ss.at[1, 0], e_rs.at[1, kk], partner).wait_recv()
        upd_ref[:, kk * HALF:(kk + 1) * HALF] = L[kk] + (R[0, kk] + R[1, kk])

    for copy in sent0 + sent1 + sent2 + shared0 + shared1 + f_sends:
        copy.wait_send()
    for p in range(2):
        for t in range(1, 4):
            ring_send(p, t, z).wait_send()
            mate_send(p, t, z).wait_send()
        ring_send_part(p, z).wait_send()
        mate_send_part(p, z).wait_send()
    for cc in range(2):
        over(cc, z).wait_send()
        merged(cc, z).wait_send()
        direct(cc, z).wait_send()
    local(z).wait_send()


def body(head_deflections, diag_inverse, coupling, panel_factor, trailing):
    h = jnp.transpose(head_deflections.reshape(V, 2, W), (1, 0, 2))
    rows = panel_factor.shape[0]
    any_spec = pl.BlockSpec(memory_space=pl.ANY)
    vmem = pl.BlockSpec(memory_space=pltpu.VMEM)
    dma = pltpu.SemaphoreType.DMA
    solved, moved = pl.pallas_call(
        kernel,
        out_shape=(
            jax.ShapeDtypeStruct((2, V, W), F32),
            jax.ShapeDtypeStruct((4 * V, rows), F32),
        ),
        in_specs=[vmem, any_spec, any_spec, any_spec],
        out_specs=(vmem, vmem),
        scratch_shapes=[
            pltpu.VMEM((2, 1024, W), F32),
            pltpu.VMEM((1024, W), F32),
            pltpu.VMEM((2, 2, HALF, W), F32),
            pltpu.VMEM((2, 2 * W, HALF), BF16),
            pltpu.VMEM((2, 2 * W, HALF), BF16),
            pltpu.VMEM((3, NC, V, W), F32),
            pltpu.VMEM((3, NC, V, W), F32),
            pltpu.VMEM((2, NZ, 2, NY, V, W), F32),
            pltpu.VMEM((NC, 4 * V, HALF), F32),
            pltpu.VMEM((2, 4 * V, HALF), F32),
            pltpu.VMEM((2, 2, 4 * V, HALF), F32),
            pltpu.VMEM((2, 4 * V, HALF), F32),
            dma((5,)), dma((2,)), dma((2,)),
            dma((3, NC)), dma((3, NC)),
            dma((2, 7)), dma((2, 7)),
            dma((2, 5)), dma((2, 5)),
            dma((2, 5)), dma((2, 5)),
            dma((4, 2)), dma((4, 2)),
        ],
        compiler_params=pltpu.CompilerParams(
            collective_id=0, has_side_effects=True, vmem_limit_bytes=32 << 20),
    )(h, diag_inverse, coupling, panel_factor)
    rest = trailing - moved.reshape(trailing.shape)
    out = jnp.transpose(solved, (1, 0, 2)).reshape(head_deflections.shape)
    return (out, rest)


def solution(mesh):
    placed = (
        P("row", None, None, "col"),
        P(None, None, "col"),
        P(None, "col"),
        P("row", None, "col"),
        P("col", None, "row"),
    )
    return jax.shard_map(
        body,
        mesh=mesh,
        in_specs=placed,
        out_specs=(P("row", None, None, "col"), P("col", None, "row")),
        check_vma=False,
    )
```

```python
import functools

import jax
import jax.numpy as jnp
from jax import lax
from jax.experimental import pallas as pl
from jax.experimental.pallas import tpu as pltpu
from jax.sharding import PartitionSpec as P

MESH = pl.DeviceIdType.MESH
F32 = jnp.float32
BF16 = jnp.bfloat16
NX, NY, NZ = 4, 4, 8
NC = 8
V = 24
W = 128
HALF = 512
LAG = 3
NT = (((1,), (1,)), ((), ()))


def split(value):
    high = value.astype(BF16)
    return high, (value - high.astype(F32)).astype(BF16)


def kernel(h_ref, d_ref, c_ref, f_ref, sol_ref, upd_ref,
           h_buf, d_buf, c_buf, f_buf, ft_hi, ft_lo, part, got, S, acc, M, R, L,
           h_sem, load_sem, fs, fr, a_ss, a_rs, y_ss, y_rs, z_ss, z_rs, p_ss, p_rs, e_ss, e_rs):
    row, col = lax.axis_index("row"), lax.axis_index("col")
    z, y = row // NY, row % NY
    x, k = col // 2, col % 2
    step_k = 1 - 2 * k
    mate = x * 2 + 1 - k
    next_z = (z + step_k + NZ) % NZ
    prev_z = (z - step_k + NZ) % NZ

    def place(zz, yy):
        return zz * NY + yy

    def remote(src, dst, ss, rs, to):
        return pltpu.make_async_remote_copy(
            src_ref=src, dst_ref=dst, send_sem=ss, recv_sem=rs, device_id=to, device_id_type=MESH)

    partner = (row, mate)
    ring_to = (place(next_z, y), col)

    barrier = pltpu.get_barrier_semaphore()
    friends = [(row, (col + o) % NC) for o in range(1, NC)]
    y_list = [(dy, dk) for dy in range(NY) for dk in range(2) if (dy, dk) != (0, 0)]
    y_dev = [(place(z, (y + dy) % NY), x * 2 + (k + dk) % 2) for dy, dk in y_list]
    friends += [dev for (dy, dk), dev in zip(y_list, y_dev) if dy]
    friends += [ring_to, (place(prev_z, y), col)]
    for dev in friends:
        pl.semaphore_signal(barrier, inc=1, device_id=dev, device_id_type=MESH)

    loads = [
        pltpu.make_async_copy(d_ref.at[0], d_buf.at[0], load_sem.at[0]),
        pltpu.make_async_copy(c_ref, c_buf, load_sem.at[1]),
        pltpu.make_async_copy(d_ref.at[1], d_buf.at[1], load_sem.at[2]),
    ]
    mine = pl.ds(pl.multiple_of(k * HALF, HALF), HALF)
    theirs = pl.ds(pl.multiple_of((1 - k) * HALF, HALF), HALF)
    for p in range(2):
        loads.append(pltpu.make_async_copy(f_ref.at[mine, p], f_buf.at[p, k], load_sem.at[3 + p]))
    heads = [
        pltpu.make_async_copy(h_ref.at[:, comp, p], h_buf.at[p, comp * 8:(comp + 1) * 8], h_sem.at[p, comp])
        for p in range(2) for comp in range(3)
    ]
    for load in heads + loads:
        load.start()

    def partial(stage, value, matrix):
        hi, lo = split(value)
        both = jnp.concatenate([hi, lo], axis=0)
        for b in range(NC):
            m_hi, m_lo = split(matrix[b * W:(b + 1) * W, :])
            one = lax.dot_general(both, m_hi, NT, preferred_element_type=F32)
            two = lax.dot_general(hi, m_lo, NT, preferred_element_type=F32)
            part[stage, b] = one[:V] + (one[V:] + two)

    def exchange(stage):
        copies = []
        for o in range(1, NC):
            to = (col + o) % NC
            copies.append(remote(part.at[stage, to], got.at[stage, o], a_ss.at[stage, o], a_rs.at[stage, o], (row, to)))
        for copy in copies:
            copy.start()
        return copies

    def collect(stage, copies):
        total = part[stage, col]
        for o in range(1, NC):
            copies[o - 1].wait_recv()
            total = total + got[stage, o]
        return total

    def share(p):
        copies = []
        for i, dev in enumerate(y_dev):
            here = S.at[p, z, k, y]
            copies.append(remote(here, here, y_ss.at[p, i], y_rs.at[p, i], dev))
        for copy in copies:
            copy.start()
        return copies

    def chunk(i):
        t = (i + 1) // 2
        sign = jnp.where(i % 2 == 1, -step_k, step_k)
        return (z + sign * t + NZ) % NZ

    def ring_send(p, t, c):
        return remote(S.at[p, c], S.at[p, c], z_ss.at[p, t], z_rs.at[p, t], ring_to)

    def ring_send_part(p, c):
        return remote(S.at[p, c, k], S.at[p, c, k], z_ss.at[p, 4], z_rs.at[p, 4], ring_to)

    def mate_send(p, t, c):
        return remote(S.at[p, c], S.at[p, c], p_ss.at[p, t], p_rs.at[p, t], partner)

    def mate_send_part(p, c):
        return remote(S.at[p, c, k], S.at[p, c, k], p_ss.at[p, 4], p_rs.at[p, 4], partner)

    def arrive(p, i):
        t = (i + 1) // 2
        c = chunk(i)

        @pl.when((i % 2 == 1) & (i < 7))
        def _():
            ring_send(p, t, c).wait_recv()

            @pl.when(i < 5)
            def _():
                ring_send(p, t + 1, c).start()

            @pl.when(i == 5)
            def _():
                ring_send_part(p, c).start()

            mate_send(p, t, c).start()

        @pl.when((i % 2 == 0) & (i > 0))
        def _():
            mate_send(p, t, c).wait_recv()

        @pl.when(i == 7)
        def _():
            ring_send_part(p, c).wait_recv()
            mate_send_part(p, c).start()
            mate_send_part(p, c).wait_recv()

    def update(p, c):
        s = jnp.concatenate([S[p, c, 0].reshape(4 * V, W), S[p, c, 1].reshape(4 * V, W)], axis=1)
        hi, lo = split(s)
        one = jnp.dot(jnp.concatenate([hi, lo], axis=0), ft_hi[p], preferred_element_type=F32)
        two = jnp.dot(hi, ft_lo[p], preferred_element_type=F32)
        return one[:4 * V] + (one[4 * V:] + two)

    for load in heads:
        load.wait()
    loads[0].wait()
    partial(0, h_buf[0], d_buf.at[0])
    pl.semaphore_wait(barrier, len(friends))
    sent0 = exchange(0)
    f_sends = [remote(f_ref.at[theirs, p], f_buf.at[p, k], fs.at[p], fr.at[p], partner) for p in range(2)]
    for copy in f_sends:
        copy.start()
    loads[1].wait()
    loads[2].wait()
    first = collect(0, sent0)
    sol_ref[0] = first
    S[0, z, k, y] = first
    partial(1, first, c_buf)
    sent1 = exchange(1)
    shared0 = share(0)

    for p in range(2):
        loads[3 + p].wait()
        f_sends[p].wait_recv()
        for kk in range(2):
            hi, lo = split(f_buf[p, kk].T)
            ft_hi[p, kk * W:(kk + 1) * W, :] = hi
            ft_lo[p, kk * W:(kk + 1) * W, :] = lo

    carried = h_buf[1] - collect(1, sent1)
    partial(2, carried, d_buf.at[1])
    sent2 = exchange(2)
    for copy in shared0:
        copy.wait_recv()
    ring_send(0, 1, z).start()
    acc[z] = update(0, z)
    second = collect(2, sent2)
    sol_ref[1] = second
    S[1, z, k, y] = second
    shared1 = share(1)

    def first_loop(i, carry):
        arrive(0, i)
        c = chunk(i)
        acc[c] = update(0, c)
        return carry

    lax.fori_loop(1, 8, first_loop, 0)
    for copy in shared1:
        copy.wait_recv()
    ring_send(1, 1, z).start()

    up = (x + step_k + NX) % NX
    down = (x - step_k + NX) % NX

    def over(cc, c):
        return remote(acc.at[c], M.at[cc], e_ss.at[0, cc], e_rs.at[0, cc], (row, up * 2 + k))

    def merged(cc, c):
        return remote(acc.at[c], R.at[0, k], e_ss.at[1, cc], e_rs.at[1, k], (row, up * 2 + cc))

    def direct(cc, c):
        return remote(acc.at[c], R.at[1, k], e_ss.at[2, cc], e_rs.at[2, k], (row, down * 2 + cc))

    def local(c):
        return remote(acc.at[c], L.at[k], e_ss.at[3, 0], e_rs.at[3, 0], partner)

    def merge(i):
        c = chunk(i)
        cc = c % 2

        @pl.when(c // 2 == up)
        def _():
            over(cc, c).wait_recv()
            acc[c] = acc[c] + M[cc]
            merged(cc, c).start()

    def second_loop(i, carry):
        arrive(1, i)
        c = chunk(i)
        acc[c] = acc[c] + update(1, c)
        to, cc = c // 2, c % 2

        @pl.when((to != up) & (to != down) & (to != x))
        def _():
            over(cc, c).start()

        @pl.when(to == down)
        def _():
            direct(cc, c).start()

        @pl.when((to == x) & (cc != k))
        def _():
            local(c).start()

        @pl.when((to == x) & (cc == k))
        def _():
            L[k] = acc[c]

        @pl.when(i >= LAG)
        def _():
            merge(i - LAG)

        return carry

    lax.fori_loop(0, 8, second_loop, 0)

    def last_loop(i, carry):
        merge(i)
        return carry

    lax.fori_loop(8 - LAG, 8, last_loop, 0)

    local(z).wait_recv()
    for kk in range(2):
        remote(acc.at[0], R.at[1, kk], e_ss.at[2, 0], e_rs.at[2, kk], partner).wait_recv()
        remote(acc.at[0], R.at[0, kk], e_ss.at[1, 0], e_rs.at[1, kk], partner).wait_recv()
        moved = L[kk] + (R[0, kk] + R[1, kk])
        for yy in range(NY):
            for comp in range(3):
                at = yy * V + comp * 8
                upd_ref[comp, yy * 8:(yy + 1) * 8, kk * HALF:(kk + 1) * HALF] = moved[at:at + 8]

    for copy in sent0 + sent1 + sent2 + shared0 + shared1 + f_sends:
        copy.wait_send()
    for p in range(2):
        for t in range(1, 4):
            ring_send(p, t, z).wait_send()
            mate_send(p, t, z).wait_send()
        ring_send_part(p, z).wait_send()
        mate_send_part(p, z).wait_send()
    for cc in range(2):
        over(cc, z).wait_send()
        merged(cc, z).wait_send()
        direct(cc, z).wait_send()
    local(z).wait_send()


def body(head_deflections, diag_inverse, coupling, panel_factor, trailing):
    rows = panel_factor.shape[0]
    any_spec = pl.BlockSpec(memory_space=pl.ANY)
    vmem = pl.BlockSpec(memory_space=pltpu.VMEM)
    dma = pltpu.SemaphoreType.DMA
    solved, moved = pl.pallas_call(
        kernel,
        out_shape=(
            jax.ShapeDtypeStruct((2, V, W), F32),
            jax.ShapeDtypeStruct((3, 4 * 8, rows), F32),
        ),
        in_specs=[any_spec] * 4,
        out_specs=(vmem, vmem),
        scratch_shapes=[
            pltpu.VMEM((2, V, W), F32),
            pltpu.VMEM((2, 1024, W), F32),
            pltpu.VMEM((1024, W), F32),
            pltpu.VMEM((2, 2, HALF, W), F32),
            pltpu.VMEM((2, 2 * W, HALF), BF16),
            pltpu.VMEM((2, 2 * W, HALF), BF16),
            pltpu.VMEM((3, NC, V, W), F32),
            pltpu.VMEM((3, NC, V, W), F32),
            pltpu.VMEM((2, NZ, 2, NY, V, W), F32),
            pltpu.VMEM((NC, 4 * V, HALF), F32),
            pltpu.VMEM((2, 4 * V, HALF), F32),
            pltpu.VMEM((2, 2, 4 * V, HALF), F32),
            pltpu.VMEM((2, 4 * V, HALF), F32),
            dma((2, 3)), dma((5,)), dma((2,)), dma((2,)),
            dma((3, NC)), dma((3, NC)),
            dma((2, 7)), dma((2, 7)),
            dma((2, 5)), dma((2, 5)),
            dma((2, 5)), dma((2, 5)),
            dma((4, 2)), dma((4, 2)),
        ],
        compiler_params=pltpu.CompilerParams(
            collective_id=0, has_side_effects=True, vmem_limit_bytes=60 << 20),
    )(head_deflections, diag_inverse, coupling, panel_factor)
    rest = trailing - jnp.transpose(moved, (1, 0, 2))
    out = jnp.transpose(solved.reshape(2, 3, 8, W), (2, 1, 0, 3))
    return (out, rest)


def solution(mesh):
    placed = (
        P("row", None, None, "col"),
        P(None, None, "col"),
        P(None, "col"),
        P("row", None, "col"),
        P("col", None, "row"),
    )
    return jax.shard_map(
        body,
        mesh=mesh,
        in_specs=placed,
        out_specs=(P("row", None, None, "col"), P("col", None, "row")),
        check_vma=False,
    )
```

```python
import functools

import jax
import jax.numpy as jnp
from jax import lax
from jax.experimental import pallas as pl
from jax.experimental.pallas import tpu as pltpu
from jax.sharding import PartitionSpec as P

MESH = pl.DeviceIdType.MESH
F32 = jnp.float32
BF16 = jnp.bfloat16
NX, NY, NZ = 4, 4, 8
NC = 8
V = 24
W = 128
HALF = 512
LAG = 4
SPANS = (((0, 8),), ((0, 1), (1, 3), (3, 5), (5, 8)))
NT = (((1,), (1,)), ((), ()))


def split(value):
    high = value.astype(BF16)
    return high, (value - high.astype(F32)).astype(BF16)


def kernel(h_ref, d_ref, c_ref, f_ref, sol_ref, upd_ref,
           h_buf, d_buf, c_buf, f_buf, ft_hi, ft_lo, part, got, S, acc, M, R, L,
           h_sem, load_sem, fs, fr, a_ss, a_rs, z_ss, z_rs, y_ss, y_rs, p_ss, p_rs, e_ss, e_rs):
    row, col = lax.axis_index("row"), lax.axis_index("col")
    z, y = row // NY, row % NY
    x, k = col // 2, col % 2
    step_k = 1 - 2 * k
    mate = x * 2 + 1 - k

    def place(zz, yy):
        return zz * NY + yy

    def remote(src, dst, ss, rs, to):
        return pltpu.make_async_remote_copy(
            src_ref=src, dst_ref=dst, send_sem=ss, recv_sem=rs, device_id=to, device_id_type=MESH)

    partner = (row, mate)

    barrier = pltpu.get_barrier_semaphore()
    friends = [(row, (col + o) % NC) for o in range(1, NC)]
    friends += [(place(z, (y + dy) % NY), col) for dy in range(1, NY)]
    friends += [(place((z + dz) % NZ, y), col) for dz in range(1, NZ)]
    for dev in friends:
        pl.semaphore_signal(barrier, inc=1, device_id=dev, device_id_type=MESH)

    loads = [
        pltpu.make_async_copy(d_ref.at[0], d_buf.at[0], load_sem.at[0]),
        pltpu.make_async_copy(c_ref, c_buf, load_sem.at[1]),
        pltpu.make_async_copy(d_ref.at[1], d_buf.at[1], load_sem.at[2]),
    ]
    mine = pl.ds(pl.multiple_of(k * HALF, HALF), HALF)
    theirs = pl.ds(pl.multiple_of((1 - k) * HALF, HALF), HALF)
    for p in range(2):
        loads.append(pltpu.make_async_copy(f_ref.at[mine, p], f_buf.at[p, k], load_sem.at[3 + p]))
    heads = [
        pltpu.make_async_copy(h_ref.at[:, comp, p], h_buf.at[p, comp * 8:(comp + 1) * 8], h_sem.at[p, comp])
        for p in range(2) for comp in range(3)
    ]
    for load in heads + loads:
        load.start()

    def partial(stage, value, matrix):
        hi, lo = split(value)
        both = jnp.concatenate([hi, lo], axis=0)
        for b in range(NC):
            m_hi, m_lo = split(matrix[b * W:(b + 1) * W, :])
            one = lax.dot_general(both, m_hi, NT, preferred_element_type=F32)
            two = lax.dot_general(hi, m_lo, NT, preferred_element_type=F32)
            part[stage, b] = one[:V] + (one[V:] + two)

    def exchange(stage):
        copies = []
        for o in range(1, NC):
            to = (col + o) % NC
            copies.append(remote(part.at[stage, to], got.at[stage, o], a_ss.at[stage, o], a_rs.at[stage, o], (row, to)))
        for copy in copies:
            copy.start()
        return copies

    def collect(stage, copies):
        total = part[stage, col]
        for o in range(1, NC):
            copies[o - 1].wait_recv()
            total = total + got[stage, o]
        return total

    def share_z(p):
        copies = []
        for i in range(1, NZ):
            dz = (i + 1) // 2 if i % 2 == 1 else NZ - i // 2
            there = (place((z + dz) % NZ, y), col)
            copies.append(remote(S.at[p, 0, k, y], S.at[p, i, k, y], z_ss.at[p, i], z_rs.at[p, i], there))
        for copy in copies:
            copy.start()
        return copies

    def share_y(p, n):
        low, high = SPANS[p][n]
        copies = []
        for dy in range(1, NY):
            block = S.at[p, pl.ds(low, high - low), k, y]
            there = (place(z, (y + dy) % NY), col)
            copies.append(remote(block, block, y_ss.at[p, n, dy], y_rs.at[p, n, dy], there))
        return copies

    def share_mate(p, n):
        low, high = SPANS[p][n]
        block = S.at[p, pl.ds(low, high - low), k]
        return remote(block, block, p_ss.at[p, n], p_rs.at[p, n], partner)

    def chunk(i):
        t = (i + 1) // 2
        return (z + jnp.where(i % 2 == 1, NZ - t, t)) % NZ

    def update(p, c):
        s = jnp.concatenate([S[p, c, 0].reshape(4 * V, W), S[p, c, 1].reshape(4 * V, W)], axis=1)
        hi, lo = split(s)
        one = jnp.dot(jnp.concatenate([hi, lo], axis=0), ft_hi[p], preferred_element_type=F32)
        two = jnp.dot(hi, ft_lo[p], preferred_element_type=F32)
        return one[:4 * V] + (one[4 * V:] + two)

    for load in heads:
        load.wait()
    loads[0].wait()
    partial(0, h_buf[0], d_buf.at[0])
    pl.semaphore_wait(barrier, len(friends))
    sent0 = exchange(0)
    f_sends = [remote(f_ref.at[theirs, p], f_buf.at[p, k], fs.at[p], fr.at[p], partner) for p in range(2)]
    for copy in f_sends:
        copy.start()
    loads[1].wait()
    loads[2].wait()
    first = collect(0, sent0)
    sol_ref[0] = first
    S[0, 0, k, y] = first
    partial(1, first, c_buf)
    sent1 = exchange(1)
    z0_sent = share_z(0)

    for p in range(2):
        loads[3 + p].wait()
        f_sends[p].wait_recv()
        for kk in range(2):
            hi, lo = split(f_buf[p, kk].T)
            ft_hi[p, kk * W:(kk + 1) * W, :] = hi
            ft_lo[p, kk * W:(kk + 1) * W, :] = lo

    carried = h_buf[1] - collect(1, sent1)
    partial(2, carried, d_buf.at[1])
    sent2 = exchange(2)
    for copy in z0_sent:
        copy.wait_recv()
    for copy in share_y(0, 0):
        copy.start()
    second = collect(2, sent2)
    sol_ref[1] = second
    S[1, 0, k, y] = second
    spans = range(len(SPANS[1]))
    for copy in share_y(1, 0):
        copy.start()
    z1_sent = share_z(1)
    for copy in share_y(0, 0):
        copy.wait_recv()
    share_mate(0, 0).start()
    for n in spans[1:]:
        for i in range(*SPANS[1][n]):
            z1_sent[i - 1].wait_recv()
        for copy in share_y(1, n):
            copy.start()
    share_mate(0, 0).wait_recv()

    def first_loop(i, carry):
        acc[i] = update(0, i)
        return carry

    lax.fori_loop(0, 8, first_loop, 0)

    up = (x + step_k + NX) % NX
    down = (x - step_k + NX) % NX

    def over(cc, i):
        return remote(acc.at[i], M.at[cc], e_ss.at[0, cc], e_rs.at[0, cc], (row, up * 2 + k))

    def merged(cc, i):
        return remote(acc.at[i], R.at[0, k], e_ss.at[1, cc], e_rs.at[1, k], (row, up * 2 + cc))

    def direct(cc, i):
        return remote(acc.at[i], R.at[1, k], e_ss.at[2, cc], e_rs.at[2, k], (row, down * 2 + cc))

    def local(i):
        return remote(acc.at[i], L.at[k], e_ss.at[3, 0], e_rs.at[3, 0], partner)

    def merge(i):
        c = chunk(i)
        cc = c % 2

        @pl.when(c // 2 == up)
        def _():
            over(cc, i).wait_recv()
            acc[i] = acc[i] + M[cc]
            merged(cc, i).start()

    def second_loop(i, carry):
        for n in spans:
            @pl.when(i == SPANS[1][n][0])
            def _():
                for copy in share_y(1, n):
                    copy.wait_recv()
                share_mate(1, n).start()
                share_mate(1, n).wait_recv()

        c = chunk(i)
        acc[i] = acc[i] + update(1, i)
        to, cc = c // 2, c % 2

        @pl.when((to != up) & (to != down) & (to != x))
        def _():
            over(cc, i).start()

        @pl.when(to == down)
        def _():
            direct(cc, i).start()

        @pl.when((to == x) & (cc != k))
        def _():
            local(i).start()

        @pl.when((to == x) & (cc == k))
        def _():
            L[k] = acc[i]

        @pl.when(i >= LAG)
        def _():
            merge(i - LAG)

        return carry

    lax.fori_loop(0, 8, second_loop, 0)

    def last_loop(i, carry):
        merge(i)
        return carry

    lax.fori_loop(8 - LAG, 8, last_loop, 0)

    local(0).wait_recv()
    for kk in range(2):
        remote(acc.at[0], R.at[1, kk], e_ss.at[2, 0], e_rs.at[2, kk], partner).wait_recv()
        remote(acc.at[0], R.at[0, kk], e_ss.at[1, 0], e_rs.at[1, kk], partner).wait_recv()
        moved = L[kk] + (R[0, kk] + R[1, kk])
        for yy in range(NY):
            for comp in range(3):
                at = yy * V + comp * 8
                upd_ref[comp, yy * 8:(yy + 1) * 8, kk * HALF:(kk + 1) * HALF] = moved[at:at + 8]

    for copy in sent0 + sent1 + sent2 + z0_sent + z1_sent + f_sends:
        copy.wait_send()
    for p in range(2):
        for n in range(len(SPANS[p])):
            for copy in share_y(p, n):
                copy.wait_send()
            share_mate(p, n).wait_send()
    for cc in range(2):
        over(cc, 0).wait_send()
        merged(cc, 0).wait_send()
        direct(cc, 0).wait_send()
    local(0).wait_send()


def body(head_deflections, diag_inverse, coupling, panel_factor, trailing):
    rows = panel_factor.shape[0]
    any_spec = pl.BlockSpec(memory_space=pl.ANY)
    vmem = pl.BlockSpec(memory_space=pltpu.VMEM)
    dma = pltpu.SemaphoreType.DMA
    solved, moved = pl.pallas_call(
        kernel,
        out_shape=(
            jax.ShapeDtypeStruct((2, V, W), F32),
            jax.ShapeDtypeStruct((3, 4 * 8, rows), F32),
        ),
        in_specs=[any_spec] * 4,
        out_specs=(vmem, vmem),
        scratch_shapes=[
            pltpu.VMEM((2, V, W), F32),
            pltpu.VMEM((2, 1024, W), F32),
            pltpu.VMEM((1024, W), F32),
            pltpu.VMEM((2, 2, HALF, W), F32),
            pltpu.VMEM((2, 2 * W, HALF), BF16),
            pltpu.VMEM((2, 2 * W, HALF), BF16),
            pltpu.VMEM((3, NC, V, W), F32),
            pltpu.VMEM((3, NC, V, W), F32),
            pltpu.VMEM((2, NZ, 2, NY, V, W), F32),
            pltpu.VMEM((NC, 4 * V, HALF), F32),
            pltpu.VMEM((2, 4 * V, HALF), F32),
            pltpu.VMEM((2, 2, 4 * V, HALF), F32),
            pltpu.VMEM((2, 4 * V, HALF), F32),
            dma((2, 3)), dma((5,)), dma((2,)), dma((2,)),
            dma((3, NC)), dma((3, NC)),
            dma((2, NZ)), dma((2, NZ)),
            dma((2, 4, NY)), dma((2, 4, NY)),
            dma((2, 4)), dma((2, 4)),
            dma((4, 2)), dma((4, 2)),
        ],
        compiler_params=pltpu.CompilerParams(
            collective_id=0, has_side_effects=True, vmem_limit_bytes=60 << 20),
    )(head_deflections, diag_inverse, coupling, panel_factor)
    rest = trailing - jnp.transpose(moved, (1, 0, 2))
    out = jnp.transpose(solved.reshape(2, 3, 8, W), (2, 1, 0, 3))
    return (out, rest)


def solution(mesh):
    placed = (
        P("row", None, None, "col"),
        P(None, None, "col"),
        P(None, "col"),
        P("row", None, "col"),
        P("col", None, "row"),
    )
    return jax.shard_map(
        body,
        mesh=mesh,
        in_specs=placed,
        out_specs=(P("row", None, None, "col"), P("col", None, "row")),
        check_vma=False,
    )
```

```python
import functools

import jax
import jax.numpy as jnp
from jax import lax
from jax.experimental import pallas as pl
from jax.experimental.pallas import tpu as pltpu
from jax.sharding import PartitionSpec as P

MESH = pl.DeviceIdType.MESH
F32 = jnp.float32
BF16 = jnp.bfloat16
NX, NY, NZ = 4, 4, 8
NC = 8
V = 24
W = 128
HALF = 512
LAG = 2
ORDER = (1, 7, 2, 6, 3, 5, 4)
SLOT = {0: 0, 6: 1, 2: 2, 4: 3, 7: 0, 1: 1, 5: 2, 3: 3}
EVEN = (0, 6, 2, 4)
ODD = (7, 1, 5, 3)
NP = 4
NT = (((1,), (1,)), ((), ()))


def split(value):
    high = value.astype(BF16)
    return high, (value - high.astype(F32)).astype(BF16)


def kernel(h_ref, d_ref, c_ref, f_ref, sol_ref, upd_ref,
           h_buf, d_buf, c_buf, f_buf, ft_hi, ft_lo, part, got, pair, own, sol_in, S, acc, M, R,
           h_sem, load_sem, fs, fr, a_ss, a_rs, b_ss, b_rs, m_ss, m_rs, z_ss, z_rs, y_ss, y_rs, e_ss, e_rs):
    row, col = lax.axis_index("row"), lax.axis_index("col")
    z, y = row // NY, row % NY
    x, k = col // 2, col % 2
    source = z % 2 == k
    other = z % 2 != k
    partner = (row, x * 2 + 1 - k)

    def place(zz, yy):
        return zz * NY + yy

    def remote(src, dst, ss, rs, to):
        return pltpu.make_async_remote_copy(
            src_ref=src, dst_ref=dst, send_sem=ss, recv_sem=rs, device_id=to, device_id_type=MESH)

    barrier = pltpu.get_barrier_semaphore()
    friends = [(row, (col + o) % NC) for o in range(1, NC)]
    friends += [(place(z, (y + dy) % NY), col) for dy in range(1, NY)]
    friends += [(place((z + dz) % NZ, y), col) for dz in range(1, NZ)]
    for dev in friends:
        pl.semaphore_signal(barrier, inc=1, device_id=dev, device_id_type=MESH)

    loads = [
        pltpu.make_async_copy(d_ref.at[0], d_buf.at[0], load_sem.at[0]),
        pltpu.make_async_copy(c_ref, c_buf, load_sem.at[1]),
        pltpu.make_async_copy(d_ref.at[1], d_buf.at[1], load_sem.at[2]),
    ]
    for p in range(2):
        loads.append(pltpu.make_async_copy(f_ref.at[:, p], f_buf.at[p, k], load_sem.at[3 + p]))
    heads = [
        pltpu.make_async_copy(h_ref.at[:, comp, p], h_buf.at[p, comp * 8:(comp + 1) * 8], h_sem.at[p, comp])
        for p in range(2) for comp in range(3)
    ]
    for load in heads + loads:
        load.start()

    def partial(stage, value, matrix):
        hi, lo = split(value)
        both = jnp.concatenate([hi, lo], axis=0)
        for b in range(NC):
            m_hi, m_lo = split(matrix[b * W:(b + 1) * W, :])
            one = lax.dot_general(both, m_hi, NT, preferred_element_type=F32)
            two = lax.dot_general(hi, m_lo, NT, preferred_element_type=F32)
            part[stage, b] = one[:V] + (one[V:] + two)

    def exchange(stage, o):
        to = (col + o) % NC
        return remote(part.at[stage, to], got.at[stage, o], a_ss.at[stage, o], a_rs.at[stage, o], (row, to))

    for load in heads:
        load.wait()
    loads[0].wait()
    partial(0, h_buf[0], d_buf.at[0])
    pl.semaphore_wait(barrier, len(friends))
    for o in range(1, NC):
        @pl.when(col + o < NC)
        def _():
            exchange(0, o).start()
    f_sends = [remote(f_ref.at[:, p], f_buf.at[p, k], fs.at[p], fr.at[p], partner) for p in range(2)]
    for copy in f_sends:
        copy.start()
    loads[1].wait()
    loads[2].wait()
    own[...] = part[0, col]
    for o in range(1, NC):
        @pl.when(col >= o)
        def _():
            exchange(0, o).wait_recv()
            own[...] = own[...] + got[0, o]
    first = own[...]
    sol_ref[0] = first
    partial(1, first, c_buf)
    for o in range(1, NC):
        exchange(1, o).start()

    def give(p):
        return remote(own, S.at[0, 0, y, k], m_ss.at[0], m_rs.at[0], partner)

    def share_z(p, dz):
        slot = SLOT[(NZ - dz) % NZ]
        there = (place((z + dz) % NZ, y), col)
        return remote(S.at[p, 0, y], S.at[p, slot, y], z_ss.at[p, dz], z_rs.at[p, slot], there)

    def wait_z(p, i):
        def wait():
            remote(S.at[p, 0, y], S.at[p, i, y], z_ss.at[p, 1], z_rs.at[p, i], partner).wait_recv()

        if i == 0:
            pl.when(other)(wait)
        else:
            wait()

    def share_y(p, i, dy):
        block = S.at[p, i, y] if p == 1 else S.at[p, :, y]
        there = (place(z, (y + dy) % NY), col)
        return remote(block, block, y_ss.at[p, i, dy], y_rs.at[p, i, dy], there)

    def start_y(p, i):
        for dy in range(1, NY):
            share_y(p, i, dy).start()

    @pl.when(other)
    def _():
        give(0).start()

    @pl.when(source)
    def _():
        S[0, 0, y, k] = first
        remote(own, S.at[0, 0, y, 1 - k], m_ss.at[0], m_rs.at[0], partner).wait_recv()
        for dz in ORDER:
            share_z(0, dz).start()

    def turn(p):
        loads[3 + p].wait()
        f_sends[p].wait_recv()
        for kk in range(2):
            hi, lo = split(f_buf[p, kk].T)
            ft_hi[p, kk * W:(kk + 1) * W, :] = hi
            ft_lo[p, kk * W:(kk + 1) * W, :] = lo

    turn(0)

    moved = part[1, col]
    for o in range(1, NC):
        exchange(1, o).wait_recv()
        moved = moved + got[1, o]
    partial(2, h_buf[1] - moved, d_buf.at[1])

    def deliver(o):
        to = (x + o) % NX
        return remote(part.at[2, pl.ds(to * 2, 2)], pair.at[o, k], b_ss.at[o], b_rs.at[o, k], (row, to * 2 + z % 2))

    def delivered(o, kk):
        return remote(part.at[2, pl.ds(x * 2, 2)], pair.at[o, kk], b_ss.at[o], b_rs.at[o, kk], partner)

    for o in range(1, NX):
        @pl.when(x + o < NX)
        def _():
            deliver(o).start()

    @pl.when(other)
    def _():
        deliver(0).start()

    for i in range(NP):
        wait_z(0, i)
    start_y(0, 0)
    turn(1)

    def reply():
        return remote(S.at[1, 0, y, 1 - k], sol_in, m_ss.at[1], m_rs.at[1], partner)

    @pl.when(source)
    def _():
        S[1, 0, y] = part[2, pl.ds(x * 2, 2)]
        for o in range(1, NX):
            @pl.when(x >= o)
            def _():
                for kk in range(2):
                    delivered(o, kk).wait_recv()
                S[1, 0, y] = S[1, 0, y] + (pair[o, 0] + pair[o, 1])

        delivered(0, 1 - k).wait_recv()
        S[1, 0, y] = S[1, 0, y] + pair[0, 1 - k]
        start_y(1, 0)
        for dz in ORDER:
            share_z(1, dz).start()
        reply().start()
        sol_ref[1] = S[1, 0, y, k]

    def update(p, i):
        s = jnp.concatenate([S[p, i, :, 0].reshape(4 * V, W), S[p, i, :, 1].reshape(4 * V, W)], axis=1)
        hi, lo = split(s)
        both = jnp.concatenate([hi, lo], axis=0)
        parts = []
        for half in range(2):
            at = slice(half * HALF, (half + 1) * HALF)
            one = jnp.dot(both, ft_hi[p, :, at], preferred_element_type=F32)
            two = jnp.dot(hi, ft_lo[p, :, at], preferred_element_type=F32)
            parts.append(one[:4 * V] + (one[4 * V:] + two))
        return parts

    right, left = (x + 1) % NX, (x + NX - 1) % NX

    def target(i):
        return (z + jnp.where(source, EVEN[i], ODD[i])) % NZ // 2

    def over(i, half):
        to = (left if half else right) * 2 + k
        return remote(acc.at[i, half], M.at[half], e_ss.at[0, half], e_rs.at[0, half], (row, to))

    def direct(i, half):
        to = (right if half else left) * 2 + k
        return remote(acc.at[i, half], R.at[0, half], e_ss.at[1, half], e_rs.at[1, half], (row, to))

    def merged(i, half):
        to = (left if half else right) * 2 + k
        return remote(acc.at[i, half], R.at[1, half], e_ss.at[2, half], e_rs.at[2, half], (row, to))

    def finish(i):
        for dy in range(1, NY):
            share_y(1, i, dy).wait_recv()
        for half, value in enumerate(update(1, i)):
            acc[i, half] = acc[i, half] + value
        to = target(i)

        @pl.when((to - x + NX) % NX == 2)
        def _():
            over(i, 0).start()
            over(i, 1).start()

        @pl.when(to == right)
        def _():
            direct(i, 1).start()

        @pl.when(to == left)
        def _():
            direct(i, 0).start()

    def merge(i):
        to = target(i)
        for half in range(2):
            @pl.when(to == (left if half else right))
            def _():
                over(i, half).wait_recv()
                acc[i, half] = acc[i, half] + M[half]
                merged(i, half).start()

    def forward(i):
        wait_z(1, i)
        if i == 0:
            @pl.when(other)
            def _():
                start_y(1, 0)
        else:
            start_y(1, i)

    def begin(i, carry):
        for half, value in enumerate(update(0, i)):
            acc[i, half] = value
        return carry

    for dy in range(1, NY):
        share_y(0, 0, dy).wait_recv()
    forward(0)
    forward(1)
    lax.fori_loop(0, NP, begin, 0)
    forward(2)
    finish(0)
    forward(3)
    for i in range(1, NP):
        finish(i)
        if i >= LAG:
            merge(i - LAG)
    for i in range(NP - LAG, NP):
        merge(i)

    mine = sum(jnp.where(target(i) == x, i, 0) for i in range(NP))
    for half in range(2):
        direct(0, half).wait_recv()
        merged(0, half).wait_recv()
        value = acc[mine, half] + (R[0, half] + R[1, half])
        for yy in range(NY):
            for comp in range(3):
                at = yy * V + comp * 8
                upd_ref[comp, yy * 8:(yy + 1) * 8, half * HALF:(half + 1) * HALF] = value[at:at + 8]

    @pl.when(other)
    def _():
        reply().wait_recv()
        sol_ref[1] = sol_in[...]

    for o in range(1, NC):
        @pl.when(col + o < NC)
        def _():
            exchange(0, o).wait_send()

        exchange(1, o).wait_send()
    for o in range(1, NX):
        @pl.when(x + o < NX)
        def _():
            deliver(o).wait_send()

    @pl.when(other)
    def _():
        deliver(0).wait_send()
        give(0).wait_send()

    @pl.when(source)
    def _():
        reply().wait_send()
        for p in range(2):
            for dz in ORDER:
                share_z(p, dz).wait_send()

    for dy in range(1, NY):
        share_y(0, 0, dy).wait_send()
        for i in range(NP):
            share_y(1, i, dy).wait_send()
    for copy in f_sends:
        copy.wait_send()
    for half in range(2):
        over(0, half).wait_send()
        direct(0, half).wait_send()
        merged(0, half).wait_send()


def body(head_deflections, diag_inverse, coupling, panel_factor, trailing):
    rows = panel_factor.shape[0]
    any_spec = pl.BlockSpec(memory_space=pl.ANY)
    vmem = pl.BlockSpec(memory_space=pltpu.VMEM)
    dma = pltpu.SemaphoreType.DMA
    solved, moved = pl.pallas_call(
        kernel,
        out_shape=(
            jax.ShapeDtypeStruct((2, V, W), F32),
            jax.ShapeDtypeStruct((3, 4 * 8, rows), F32),
        ),
        in_specs=[any_spec] * 4,
        out_specs=(vmem, vmem),
        scratch_shapes=[
            pltpu.VMEM((2, V, W), F32),
            pltpu.VMEM((2, 1024, W), F32),
            pltpu.VMEM((1024, W), F32),
            pltpu.VMEM((2, 2, rows, W), F32),
            pltpu.VMEM((2, 2 * W, rows), BF16),
            pltpu.VMEM((2, 2 * W, rows), BF16),
            pltpu.VMEM((3, NC, V, W), F32),
            pltpu.VMEM((2, NC, V, W), F32),
            pltpu.VMEM((NX, 2, 2, V, W), F32),
            pltpu.VMEM((V, W), F32),
            pltpu.VMEM((V, W), F32),
            pltpu.VMEM((2, NP, NY, 2, V, W), F32),
            pltpu.VMEM((NP, 2, 4 * V, HALF), F32),
            pltpu.VMEM((2, 4 * V, HALF), F32),
            pltpu.VMEM((2, 2, 4 * V, HALF), F32),
            dma((2, 3)), dma((5,)), dma((2,)), dma((2,)),
            dma((2, NC)), dma((2, NC)),
            dma((NX,)), dma((NX, 2)),
            dma((2,)), dma((2,)),
            dma((2, NZ)), dma((2, NP)),
            dma((2, NP, NY)), dma((2, NP, NY)),
            dma((3, 2)), dma((3, 2)),
        ],
        compiler_params=pltpu.CompilerParams(
            collective_id=0, has_side_effects=True, vmem_limit_bytes=60 << 20),
    )(head_deflections, diag_inverse, coupling, panel_factor)
    rest = trailing - jnp.transpose(moved, (1, 0, 2))
    out = jnp.transpose(solved.reshape(2, 3, 8, W), (2, 1, 0, 3))
    return (out, rest)


def solution(mesh):
    placed = (
        P("row", None, None, "col"),
        P(None, None, "col"),
        P(None, "col"),
        P("row", None, "col"),
        P("col", None, "row"),
    )
    return jax.shard_map(
        body,
        mesh=mesh,
        in_specs=placed,
        out_specs=(P("row", None, None, "col"), P("col", None, "row")),
        check_vma=False,
    )
```

```python
import functools

import jax
import jax.numpy as jnp
from jax import lax
from jax.experimental import pallas as pl
from jax.experimental.pallas import tpu as pltpu
from jax.sharding import PartitionSpec as P

MESH = pl.DeviceIdType.MESH
F32 = jnp.float32
BF16 = jnp.bfloat16
NX, NY, NZ = 4, 4, 8
NC = 8
V = 24
W = 128
HALF = 512
LAG = 3
PIECES = 2
ROWS = 4 * V // PIECES
ORDER = (1, 7, 2, 6, 3, 5, 4)
SLOT = {0: 0, 6: 1, 2: 2, 4: 3, 7: 0, 1: 1, 5: 2, 3: 3}
EVEN = (0, 6, 2, 4)
ODD = (7, 1, 5, 3)
NP = 4
NT = (((1,), (1,)), ((), ()))


def split(value):
    high = value.astype(BF16)
    return high, (value - high.astype(F32)).astype(BF16)


def kernel(h_ref, d_ref, c_ref, f_ref, sol_ref, upd_ref,
           h_buf, d_buf, c_buf, f_buf, f_turn, ft_hi, ft_lo, part, got, pair, own, sol_in, S, acc, M, R,
           h_sem, load_sem, fs, fr, a_ss, a_rs, b_ss, b_rs, m_ss, m_rs, z_ss, z_rs, y_ss, y_rs, e_ss, e_rs, o_ss, o_rs):
    row, col = lax.axis_index("row"), lax.axis_index("col")
    z, y = row // NY, row % NY
    x, k = col // 2, col % 2
    source = z % 2 == k
    other = z % 2 != k
    partner = (row, x * 2 + 1 - k)

    def place(zz, yy):
        return zz * NY + yy

    def remote(src, dst, ss, rs, to):
        return pltpu.make_async_remote_copy(
            src_ref=src, dst_ref=dst, send_sem=ss, recv_sem=rs, device_id=to, device_id_type=MESH)

    loads = [
        pltpu.make_async_copy(d_ref.at[0], d_buf.at[0], load_sem.at[0]),
        pltpu.make_async_copy(c_ref, c_buf, load_sem.at[1]),
        pltpu.make_async_copy(d_ref.at[1], d_buf.at[1], load_sem.at[2]),
    ]
    for p in range(2):
        loads.append(pltpu.make_async_copy(f_ref.at[:, p], f_buf.at[p], load_sem.at[3 + p]))
    heads = [
        pltpu.make_async_copy(h_ref.at[:, comp, p], h_buf.at[p, comp * 8:(comp + 1) * 8], h_sem.at[p, comp])
        for p in range(2) for comp in range(3)
    ]
    for load in heads + loads:
        load.start()

    barrier = pltpu.get_barrier_semaphore()
    friends = [(row, (col + o) % NC) for o in range(1, NC)]
    friends += [(place(z, (y + dy) % NY), col) for dy in range(1, NY)]
    friends += [(place((z + dz) % NZ, y), col) for dz in range(1, NZ)]
    for dev in friends:
        pl.semaphore_signal(barrier, inc=1, device_id=dev, device_id_type=MESH)

    def partial(stage, value, matrix):
        hi, lo = split(value)
        both = jnp.concatenate([hi, lo], axis=0)
        for b in range(NC):
            m_hi, m_lo = split(matrix[b * W:(b + 1) * W, :])
            one = lax.dot_general(both, m_hi, NT, preferred_element_type=F32)
            two = lax.dot_general(hi, m_lo, NT, preferred_element_type=F32)
            part[stage, b] = one[:V] + (one[V:] + two)

    def exchange(stage, o):
        to = (col + o) % NC
        return remote(part.at[stage, to], got.at[stage, o], a_ss.at[stage, o], a_rs.at[stage, o], (row, to))

    for load in heads:
        load.wait()
    loads[0].wait()
    partial(0, h_buf[0], d_buf.at[0])
    for p in range(2):
        loads[3 + p].wait()
        f_turn[p, k] = f_buf[p].T
    pl.semaphore_wait(barrier, len(friends))
    for o in range(1, NC):
        @pl.when(col + o < NC)
        def _():
            exchange(0, o).start()
    f_sends = [remote(f_turn.at[p, k], f_turn.at[p, k], fs.at[p], fr.at[p], partner) for p in range(2)]
    for copy in f_sends:
        copy.start()
    loads[1].wait()
    loads[2].wait()
    own[...] = part[0, col]
    for o in range(1, NC):
        @pl.when(col >= o)
        def _():
            exchange(0, o).wait_recv()
            own[...] = own[...] + got[0, o]
    first = own[...]
    sol_ref[0] = first
    partial(1, first, c_buf)
    for o in range(1, NC):
        exchange(1, o).start()

    def give(p):
        return remote(own, S.at[0, 0, y, k], m_ss.at[0], m_rs.at[0], partner)

    def share_z(p, dz):
        slot = SLOT[(NZ - dz) % NZ]
        there = (place((z + dz) % NZ, y), col)
        return remote(S.at[p, 0, y], S.at[p, slot, y], z_ss.at[p, dz], z_rs.at[p, slot], there)

    def wait_z(p, i):
        def wait():
            remote(S.at[p, 0, y], S.at[p, i, y], z_ss.at[p, 1], z_rs.at[p, i], partner).wait_recv()

        if i == 0:
            pl.when(other)(wait)
        else:
            wait()

    def share_y(p, i, dy):
        block = S.at[p, i, y] if p == 1 else S.at[p, :, y]
        there = (place(z, (y + dy) % NY), col)
        return remote(block, block, y_ss.at[p, i, dy], y_rs.at[p, i, dy], there)

    def start_y(p, i):
        for dy in range(1, NY):
            share_y(p, i, dy).start()

    @pl.when(other)
    def _():
        give(0).start()

    @pl.when(source)
    def _():
        S[0, 0, y, k] = first
        remote(own, S.at[0, 0, y, 1 - k], m_ss.at[0], m_rs.at[0], partner).wait_recv()
        for dz in ORDER:
            share_z(0, dz).start()

    def turn(p):
        f_sends[p].wait_recv()
        for kk in range(2):
            hi, lo = split(f_turn[p, kk])
            ft_hi[p, kk * W:(kk + 1) * W, :] = hi
            ft_lo[p, kk * W:(kk + 1) * W, :] = lo

    turn(0)

    moved = part[1, col]
    for o in range(1, NC):
        exchange(1, o).wait_recv()
        moved = moved + got[1, o]
    partial(2, h_buf[1] - moved, d_buf.at[1])

    def deliver(o):
        to = (x + o) % NX
        return remote(part.at[2, pl.ds(to * 2, 2)], pair.at[o, k], b_ss.at[o], b_rs.at[o, k], (row, to * 2 + z % 2))

    def delivered(o, kk):
        return remote(part.at[2, pl.ds(x * 2, 2)], pair.at[o, kk], b_ss.at[o], b_rs.at[o, kk], partner)

    for o in range(1, NX):
        @pl.when(x + o < NX)
        def _():
            deliver(o).start()

    @pl.when(other)
    def _():
        deliver(0).start()

    for i in range(NP):
        wait_z(0, i)
    start_y(0, 0)
    turn(1)

    def reply():
        return remote(S.at[1, 0, y, 1 - k], sol_in, m_ss.at[1], m_rs.at[1], partner)

    @pl.when(source)
    def _():
        S[1, 0, y] = part[2, pl.ds(x * 2, 2)]
        for o in range(1, NX):
            @pl.when(x >= o)
            def _():
                for kk in range(2):
                    delivered(o, kk).wait_recv()
                S[1, 0, y] = S[1, 0, y] + (pair[o, 0] + pair[o, 1])

        delivered(0, 1 - k).wait_recv()
        S[1, 0, y] = S[1, 0, y] + pair[0, 1 - k]
        start_y(1, 0)
        for dz in ORDER:
            share_z(1, dz).start()
        reply().start()
        sol_ref[1] = S[1, 0, y, k]

    def update(p, i):
        s = jnp.concatenate([S[p, i, :, 0].reshape(4 * V, W), S[p, i, :, 1].reshape(4 * V, W)], axis=1)
        hi, lo = split(s)
        both = jnp.concatenate([hi, lo], axis=0)
        parts = []
        for half in range(2):
            at = slice(half * HALF, (half + 1) * HALF)
            one = jnp.dot(both, ft_hi[p, :, at], preferred_element_type=F32)
            two = jnp.dot(hi, ft_lo[p, :, at], preferred_element_type=F32)
            parts.append(one[:4 * V] + (one[4 * V:] + two))
        return parts

    right, left = (x + 1) % NX, (x + NX - 1) % NX

    def target(i):
        return (z + jnp.where(source, EVEN[i], ODD[i])) % NZ // 2

    def piece(n):
        return pl.ds(n * ROWS, ROWS)

    def over(i, half, n):
        to = (left if half else right) * 2 + k
        return remote(acc.at[i, half, piece(n)], M.at[half, piece(n)],
                      o_ss.at[0, half, n], o_rs.at[0, half, n], (row, to))

    def direct(i, half):
        to = (right if half else left) * 2 + k
        return remote(acc.at[i, half], R.at[0, half], e_ss.at[half], e_rs.at[half], (row, to))

    def merged(i, half, n):
        to = (left if half else right) * 2 + k
        return remote(acc.at[i, half, piece(n)], R.at[1, half, piece(n)],
                      o_ss.at[1, half, n], o_rs.at[1, half, n], (row, to))

    def finish(i):
        for dy in range(1, NY):
            share_y(1, i, dy).wait_recv()
        for half, value in enumerate(update(1, i)):
            acc[i, half] = acc[i, half] + value
        to = target(i)

        @pl.when((to - x + NX) % NX == 2)
        def _():
            for n in range(PIECES):
                over(i, 0, n).start()
                over(i, 1, n).start()

        @pl.when(to == right)
        def _():
            direct(i, 1).start()

        @pl.when(to == left)
        def _():
            direct(i, 0).start()

    def merge(i):
        to = target(i)
        for half in range(2):
            @pl.when(to == (left if half else right))
            def _():
                for n in range(PIECES):
                    over(i, half, n).wait_recv()
                    acc[i, half, piece(n)] = acc[i, half, piece(n)] + M[half, piece(n)]
                    merged(i, half, n).start()

    def forward(i):
        wait_z(1, i)
        if i == 0:
            @pl.when(other)
            def _():
                start_y(1, 0)
        else:
            start_y(1, i)

    def begin(i):
        for half, value in enumerate(update(0, i)):
            acc[i, half] = value

    for dy in range(1, NY):
        share_y(0, 0, dy).wait_recv()
    forward(0)
    forward(1)
    begin(0)
    forward(2)
    forward(3)
    for i in range(NP):
        if i > 0:
            begin(i)
        finish(i)
        if i >= LAG:
            merge(i - LAG)
    for i in range(NP - LAG, NP):
        merge(i)

    mine = sum(jnp.where(target(i) == x, i, 0) for i in range(NP))
    for half in range(2):
        direct(0, half).wait_recv()
    for n in range(PIECES):
        for half in range(2):
            merged(0, half, n).wait_recv()
            for unit in range(n * ROWS // 8, (n + 1) * ROWS // 8):
                yy, comp = unit // 3, unit % 3
                rows = slice(unit * 8, unit * 8 + 8)
                value = acc[mine, half, rows] + (R[0, half, rows] + R[1, half, rows])
                upd_ref[comp, yy * 8:(yy + 1) * 8, half * HALF:(half + 1) * HALF] = value

    @pl.when(other)
    def _():
        reply().wait_recv()
        sol_ref[1] = sol_in[...]

    for o in range(1, NC):
        @pl.when(col + o < NC)
        def _():
            exchange(0, o).wait_send()

        exchange(1, o).wait_send()
    for o in range(1, NX):
        @pl.when(x + o < NX)
        def _():
            deliver(o).wait_send()

    @pl.when(other)
    def _():
        deliver(0).wait_send()
        give(0).wait_send()

    @pl.when(source)
    def _():
        reply().wait_send()
        for p in range(2):
            for dz in ORDER:
                share_z(p, dz).wait_send()

    for dy in range(1, NY):
        share_y(0, 0, dy).wait_send()
        for i in range(NP):
            share_y(1, i, dy).wait_send()
    for copy in f_sends:
        copy.wait_send()
    for half in range(2):
        direct(0, half).wait_send()
        for n in range(PIECES):
            over(0, half, n).wait_send()
            merged(0, half, n).wait_send()


def body(head_deflections, diag_inverse, coupling, panel_factor, trailing):
    rows = panel_factor.shape[0]
    any_spec = pl.BlockSpec(memory_space=pl.ANY)
    vmem = pl.BlockSpec(memory_space=pltpu.VMEM)
    dma = pltpu.SemaphoreType.DMA
    solved, moved = pl.pallas_call(
        kernel,
        out_shape=(
            jax.ShapeDtypeStruct((2, V, W), F32),
            jax.ShapeDtypeStruct((3, 4 * 8, rows), F32),
        ),
        in_specs=[any_spec] * 4,
        out_specs=(vmem, vmem),
        scratch_shapes=[
            pltpu.VMEM((2, V, W), F32),
            pltpu.VMEM((2, 1024, W), F32),
            pltpu.VMEM((1024, W), F32),
            pltpu.VMEM((2, rows, W), F32),
            pltpu.VMEM((2, 2, W, rows), F32),
            pltpu.VMEM((2, 2 * W, rows), BF16),
            pltpu.VMEM((2, 2 * W, rows), BF16),
            pltpu.VMEM((3, NC, V, W), F32),
            pltpu.VMEM((2, NC, V, W), F32),
            pltpu.VMEM((NX, 2, 2, V, W), F32),
            pltpu.VMEM((V, W), F32),
            pltpu.VMEM((V, W), F32),
            pltpu.VMEM((2, NP, NY, 2, V, W), F32),
            pltpu.VMEM((NP, 2, 4 * V, HALF), F32),
            pltpu.VMEM((2, 4 * V, HALF), F32),
            pltpu.VMEM((2, 2, 4 * V, HALF), F32),
            dma((2, 3)), dma((5,)), dma((2,)), dma((2,)),
            dma((2, NC)), dma((2, NC)),
            dma((NX,)), dma((NX, 2)),
            dma((2,)), dma((2,)),
            dma((2, NZ)), dma((2, NP)),
            dma((2, NP, NY)), dma((2, NP, NY)),
            dma((2,)), dma((2,)),
            dma((2, 2, PIECES)), dma((2, 2, PIECES)),
        ],
        compiler_params=pltpu.CompilerParams(
            collective_id=0, has_side_effects=True, vmem_limit_bytes=int(53.5 * (1 << 20))),
    )(head_deflections, diag_inverse, coupling, panel_factor)
    rest = trailing - jnp.transpose(moved, (1, 0, 2))
    out = jnp.transpose(solved.reshape(2, 3, 8, W), (2, 1, 0, 3))
    return (out, rest)


def solution(mesh):
    placed = (
        P("row", None, None, "col"),
        P(None, None, "col"),
        P(None, "col"),
        P("row", None, "col"),
        P("col", None, "row"),
    )
    return jax.shard_map(
        body,
        mesh=mesh,
        in_specs=placed,
        out_specs=(P("row", None, None, "col"), P("col", None, "row")),
        check_vma=False,
    )
```

```python
import functools

import jax
import jax.numpy as jnp
from jax import lax
from jax.experimental import pallas as pl
from jax.experimental.pallas import tpu as pltpu
from jax.sharding import PartitionSpec as P

MESH = pl.DeviceIdType.MESH
F32 = jnp.float32
BF16 = jnp.bfloat16
NX, NY, NZ = 4, 4, 8
NC = 8
V = 24
W = 128
HALF = 512
LAG = 3
PIECES = 2
ROWS = 4 * V // PIECES
ORDER = (1, 7, 2, 6, 3, 5, 4)
SLOT = {0: 0, 6: 1, 2: 2, 4: 3, 7: 0, 1: 1, 5: 2, 3: 3}
EVEN = (0, 6, 2, 4)
ODD = (7, 1, 5, 3)
NP = 4
NT = (((1,), (1,)), ((), ()))


def split(value):
    high = value.astype(BF16)
    return high, (value - high.astype(F32)).astype(BF16)


def kernel(h_ref, d_ref, c_ref, f_ref, sol_ref, upd_ref,
           h_buf, d_buf, c_buf, f_buf, f_turn, ft_hi, ft_lo, part, got, pair, own, sol_in, S, acc, M, R,
           h_sem, load_sem, fs, fr, a_ss, a_rs, b_ss, b_rs, m_ss, m_rs, z_ss, z_rs, y_ss, y_rs, e_ss, e_rs, o_ss, o_rs):
    row, col = lax.axis_index("row"), lax.axis_index("col")
    z, y = row // NY, row % NY
    x, k = col // 2, col % 2
    source = z % 2 == k
    other = z % 2 != k
    partner = (row, x * 2 + 1 - k)

    def place(zz, yy):
        return zz * NY + yy

    def remote(src, dst, ss, rs, to):
        return pltpu.make_async_remote_copy(
            src_ref=src, dst_ref=dst, send_sem=ss, recv_sem=rs, device_id=to, device_id_type=MESH)

    loads = [
        pltpu.make_async_copy(d_ref.at[0], d_buf.at[0], load_sem.at[0]),
        pltpu.make_async_copy(c_ref, c_buf, load_sem.at[1]),
        pltpu.make_async_copy(d_ref.at[1], d_buf.at[1], load_sem.at[2]),
    ]
    for p in range(2):
        loads.append(pltpu.make_async_copy(f_ref.at[:, p], f_buf.at[p], load_sem.at[3 + p]))
    heads = [
        pltpu.make_async_copy(h_ref.at[:, comp, p], h_buf.at[p, comp * 8:(comp + 1) * 8], h_sem.at[p, comp])
        for p in range(2) for comp in range(3)
    ]
    for load in heads + loads:
        load.start()

    barrier = pltpu.get_barrier_semaphore()
    friends = [(row, (col + o) % NC) for o in range(1, NC)]
    friends += [(place(z, (y + dy) % NY), col) for dy in range(1, NY)]
    friends += [(place((z + dz) % NZ, y), col) for dz in range(1, NZ)]
    for dev in friends:
        pl.semaphore_signal(barrier, inc=1, device_id=dev, device_id_type=MESH)

    def partial(stage, value, matrix):
        hi, lo = split(value)
        both = jnp.concatenate([hi, lo], axis=0)
        for b in range(NC):
            m_hi, m_lo = split(matrix[b * W:(b + 1) * W, :])
            one = lax.dot_general(both, m_hi, NT, preferred_element_type=F32)
            two = lax.dot_general(hi, m_lo, NT, preferred_element_type=F32)
            part[stage, b] = one[:V] + (one[V:] + two)

    def exchange(stage, o):
        to = (col + o) % NC
        return remote(part.at[stage, to], got.at[stage, o], a_ss.at[stage, o], a_rs.at[stage, o], (row, to))

    for load in heads:
        load.wait()
    loads[0].wait()
    partial(0, h_buf[0], d_buf.at[0])
    for p in range(2):
        loads[3 + p].wait()
        f_turn[p, k] = f_buf[p].T
    pl.semaphore_wait(barrier, len(friends))
    for o in range(1, NC):
        @pl.when(col + o < NC)
        def _():
            exchange(0, o).start()
    f_sends = [remote(f_turn.at[p, k], f_turn.at[p, k], fs.at[p], fr.at[p], partner) for p in range(2)]
    for copy in f_sends:
        copy.start()
    loads[1].wait()
    loads[2].wait()
    own[...] = part[0, col]
    for o in range(1, NC):
        @pl.when(col >= o)
        def _():
            exchange(0, o).wait_recv()
            own[...] = own[...] + got[0, o]
    first = own[...]
    sol_ref[0] = first
    partial(1, first, c_buf)
    for o in range(1, NC):
        exchange(1, o).start()

    def give(p):
        return remote(own, S.at[0, 0, y, k], m_ss.at[0], m_rs.at[0], partner)

    def share_z(p, dz):
        slot = SLOT[(NZ - dz) % NZ]
        there = (place((z + dz) % NZ, y), col)
        return remote(S.at[p, 0, y], S.at[p, slot, y], z_ss.at[p, dz], z_rs.at[p, slot], there)

    def wait_z(p, i):
        def wait():
            remote(S.at[p, 0, y], S.at[p, i, y], z_ss.at[p, 1], z_rs.at[p, i], partner).wait_recv()

        if i == 0:
            pl.when(other)(wait)
        else:
            wait()

    def share_y(p, i, dy):
        block = S.at[p, i, y] if p == 1 else S.at[p, :, y]
        there = (place(z, (y + dy) % NY), col)
        return remote(block, block, y_ss.at[p, i, dy], y_rs.at[p, i, dy], there)

    def start_y(p, i):
        for dy in range(1, NY):
            share_y(p, i, dy).start()

    @pl.when(other)
    def _():
        give(0).start()

    @pl.when(source)
    def _():
        S[0, 0, y, k] = first
        remote(own, S.at[0, 0, y, 1 - k], m_ss.at[0], m_rs.at[0], partner).wait_recv()
        for dz in ORDER:
            share_z(0, dz).start()

    def turn(p):
        f_sends[p].wait_recv()
        for kk in range(2):
            hi, lo = split(f_turn[p, kk])
            ft_hi[p, kk * W:(kk + 1) * W, :] = hi
            ft_lo[p, kk * W:(kk + 1) * W, :] = lo

    turn(0)

    moved = part[1, col]
    for o in range(1, NC):
        exchange(1, o).wait_recv()
        moved = moved + got[1, o]
    partial(2, h_buf[1] - moved, d_buf.at[1])

    def deliver(o):
        to = (x + o) % NX
        return remote(part.at[2, pl.ds(to * 2, 2)], pair.at[o, k], b_ss.at[o], b_rs.at[o, k], (row, to * 2 + z % 2))

    def delivered(o, kk):
        return remote(part.at[2, pl.ds(x * 2, 2)], pair.at[o, kk], b_ss.at[o], b_rs.at[o, kk], partner)

    for o in range(1, NX):
        @pl.when(x + o < NX)
        def _():
            deliver(o).start()

    @pl.when(other)
    def _():
        deliver(0).start()

    for i in range(NP):
        wait_z(0, i)
    start_y(0, 0)
    turn(1)

    def reply():
        return remote(S.at[1, 0, y, 1 - k], sol_in, m_ss.at[1], m_rs.at[1], partner)

    @pl.when(source)
    def _():
        S[1, 0, y] = part[2, pl.ds(x * 2, 2)]
        for o in range(1, NX):
            @pl.when(x >= o)
            def _():
                for kk in range(2):
                    delivered(o, kk).wait_recv()
                S[1, 0, y] = S[1, 0, y] + (pair[o, 0] + pair[o, 1])

        delivered(0, 1 - k).wait_recv()
        S[1, 0, y] = S[1, 0, y] + pair[0, 1 - k]
        start_y(1, 0)
        for dz in ORDER:
            share_z(1, dz).start()
        reply().start()
        sol_ref[1] = S[1, 0, y, k]

    def update(p, i):
        s = jnp.concatenate([S[p, i, :, 0].reshape(4 * V, W), S[p, i, :, 1].reshape(4 * V, W)], axis=1)
        hi, lo = split(s)
        both = jnp.concatenate([hi, lo], axis=0)
        parts = []
        for half in range(2):
            at = slice(half * HALF, (half + 1) * HALF)
            one = jnp.dot(both, ft_hi[p, :, at], preferred_element_type=F32)
            two = jnp.dot(hi, ft_lo[p, :, at], preferred_element_type=F32)
            parts.append(one[:4 * V] + (one[4 * V:] + two))
        return parts

    right, left = (x + 1) % NX, (x + NX - 1) % NX

    def target(i):
        return (z + jnp.where(source, EVEN[i], ODD[i])) % NZ // 2

    def piece(n):
        return pl.ds(n * ROWS, ROWS)

    def over(i, half, n):
        to = (left if half else right) * 2 + k
        return remote(acc.at[i, half, piece(n)], M.at[half, piece(n)],
                      o_ss.at[0, half, n], o_rs.at[0, half, n], (row, to))

    def direct(i, half):
        to = (right if half else left) * 2 + k
        return remote(acc.at[i, half], R.at[0, half], e_ss.at[half], e_rs.at[half], (row, to))

    def merged(i, half, n):
        to = (left if half else right) * 2 + k
        return remote(acc.at[i, half, piece(n)], R.at[1, half, piece(n)],
                      o_ss.at[1, half, n], o_rs.at[1, half, n], (row, to))

    def finish(i):
        for dy in range(1, NY):
            share_y(1, i, dy).wait_recv()
        for half, value in enumerate(update(1, i)):
            acc[i, half] = acc[i, half] + value
        to = target(i)

        @pl.when((to - x + NX) % NX == 2)
        def _():
            for n in range(PIECES):
                over(i, 0, n).start()
                over(i, 1, n).start()

        @pl.when(to == right)
        def _():
            direct(i, 1).start()

        @pl.when(to == left)
        def _():
            direct(i, 0).start()

    def merge(i):
        to = target(i)
        for half in range(2):
            @pl.when(to == (left if half else right))
            def _():
                for n in range(PIECES):
                    over(i, half, n).wait_recv()
                    acc[i, half, piece(n)] = acc[i, half, piece(n)] + M[half, piece(n)]
                    merged(i, half, n).start()

    def forward(i):
        wait_z(1, i)
        if i == 0:
            @pl.when(other)
            def _():
                start_y(1, 0)
        else:
            start_y(1, i)

    def begin(i):
        for half, value in enumerate(update(0, i)):
            acc[i, half] = value

    for i in range(NP):
        forward(i)
    for dy in range(1, NY):
        share_y(0, 0, dy).wait_recv()
    for i in range(NP):
        begin(i)
    for i in range(NP):
        finish(i)
        if i >= LAG:
            merge(i - LAG)
    for i in range(NP - LAG, NP):
        merge(i)

    mine = sum(jnp.where(target(i) == x, i, 0) for i in range(NP))
    for half in range(2):
        direct(0, half).wait_recv()
    for n in range(PIECES):
        for half in range(2):
            merged(0, half, n).wait_recv()
            for unit in range(n * ROWS // 8, (n + 1) * ROWS // 8):
                yy, comp = unit // 3, unit % 3
                rows = slice(unit * 8, unit * 8 + 8)
                value = acc[mine, half, rows] + (R[0, half, rows] + R[1, half, rows])
                upd_ref[comp, yy * 8:(yy + 1) * 8, half * HALF:(half + 1) * HALF] = value

    @pl.when(other)
    def _():
        reply().wait_recv()
        sol_ref[1] = sol_in[...]

    for o in range(1, NC):
        @pl.when(col + o < NC)
        def _():
            exchange(0, o).wait_send()

        exchange(1, o).wait_send()
    for o in range(1, NX):
        @pl.when(x + o < NX)
        def _():
            deliver(o).wait_send()

    @pl.when(other)
    def _():
        deliver(0).wait_send()
        give(0).wait_send()

    @pl.when(source)
    def _():
        reply().wait_send()
        for p in range(2):
            for dz in ORDER:
                share_z(p, dz).wait_send()

    for dy in range(1, NY):
        share_y(0, 0, dy).wait_send()
        for i in range(NP):
            share_y(1, i, dy).wait_send()
    for copy in f_sends:
        copy.wait_send()
    for half in range(2):
        direct(0, half).wait_send()
        for n in range(PIECES):
            over(0, half, n).wait_send()
            merged(0, half, n).wait_send()


def body(head_deflections, diag_inverse, coupling, panel_factor, trailing):
    rows = panel_factor.shape[0]
    any_spec = pl.BlockSpec(memory_space=pl.ANY)
    vmem = pl.BlockSpec(memory_space=pltpu.VMEM)
    dma = pltpu.SemaphoreType.DMA
    solved, moved = pl.pallas_call(
        kernel,
        out_shape=(
            jax.ShapeDtypeStruct((2, V, W), F32),
            jax.ShapeDtypeStruct((3, 4 * 8, rows), F32),
        ),
        in_specs=[any_spec] * 4,
        out_specs=(vmem, vmem),
        scratch_shapes=[
            pltpu.VMEM((2, V, W), F32),
            pltpu.VMEM((2, 1024, W), F32),
            pltpu.VMEM((1024, W), F32),
            pltpu.VMEM((2, rows, W), F32),
            pltpu.VMEM((2, 2, W, rows), F32),
            pltpu.VMEM((2, 2 * W, rows), BF16),
            pltpu.VMEM((2, 2 * W, rows), BF16),
            pltpu.VMEM((3, NC, V, W), F32),
            pltpu.VMEM((2, NC, V, W), F32),
            pltpu.VMEM((NX, 2, 2, V, W), F32),
            pltpu.VMEM((V, W), F32),
            pltpu.VMEM((V, W), F32),
            pltpu.VMEM((2, NP, NY, 2, V, W), F32),
            pltpu.VMEM((NP, 2, 4 * V, HALF), F32),
            pltpu.VMEM((2, 4 * V, HALF), F32),
            pltpu.VMEM((2, 2, 4 * V, HALF), F32),
            dma((2, 3)), dma((5,)), dma((2,)), dma((2,)),
            dma((2, NC)), dma((2, NC)),
            dma((NX,)), dma((NX, 2)),
            dma((2,)), dma((2,)),
            dma((2, NZ)), dma((2, NP)),
            dma((2, NP, NY)), dma((2, NP, NY)),
            dma((2,)), dma((2,)),
            dma((2, 2, PIECES)), dma((2, 2, PIECES)),
        ],
        compiler_params=pltpu.CompilerParams(
            collective_id=0, has_side_effects=True, vmem_limit_bytes=int(53.5 * (1 << 20))),
    )(head_deflections, diag_inverse, coupling, panel_factor)
    rest = trailing - jnp.transpose(moved, (1, 0, 2))
    out = jnp.transpose(solved.reshape(2, 3, 8, W), (2, 1, 0, 3))
    return (out, rest)


def solution(mesh):
    placed = (
        P("row", None, None, "col"),
        P(None, None, "col"),
        P(None, "col"),
        P("row", None, "col"),
        P("col", None, "row"),
    )
    return jax.shard_map(
        body,
        mesh=mesh,
        in_specs=placed,
        out_specs=(P("row", None, None, "col"), P("col", None, "row")),
        check_vma=False,
    )
```

```python
import functools

import jax
import jax.numpy as jnp
from jax import lax
from jax.experimental import pallas as pl
from jax.experimental.pallas import tpu as pltpu
from jax.sharding import PartitionSpec as P

MESH = pl.DeviceIdType.MESH
F32 = jnp.float32
BF16 = jnp.bfloat16
NX, NY, NZ = 4, 4, 8
NC = 8
V = 24
W = 128
HALF = 512
LAG = 3
PIECES = 2
ROWS = 4 * V // PIECES
ORDER = (1, 7, 2, 6, 3, 5, 4)
SLOT = {0: 0, 6: 1, 2: 2, 4: 3, 7: 0, 1: 1, 5: 2, 3: 3}
EVEN = (0, 6, 2, 4)
ODD = (7, 1, 5, 3)
NP = 4
NT = (((1,), (1,)), ((), ()))


def split(value):
    high = value.astype(BF16)
    return high, (value - high.astype(F32)).astype(BF16)


def kernel(h_ref, d_ref, c_ref, f_ref, sol_ref, upd_ref,
           h_buf, d_buf, c_buf, f_buf, f_turn, ft_hi, ft_lo, part, got, pair, own, sol_in, S, acc, M, R,
           h_sem, load_sem, fs, fr, a_ss, a_rs, b_ss, b_rs, m_ss, m_rs, z_ss, z_rs, y_ss, y_rs, e_ss, e_rs, o_ss, o_rs):
    row, col = lax.axis_index("row"), lax.axis_index("col")
    z, y = row // NY, row % NY
    x, k = col // 2, col % 2
    source = z % 2 == k
    other = z % 2 != k
    partner = (row, x * 2 + 1 - k)

    def place(zz, yy):
        return zz * NY + yy

    def remote(src, dst, ss, rs, to):
        return pltpu.make_async_remote_copy(
            src_ref=src, dst_ref=dst, send_sem=ss, recv_sem=rs, device_id=to, device_id_type=MESH)

    loads = [
        pltpu.make_async_copy(d_ref.at[0], d_buf.at[0], load_sem.at[0]),
        pltpu.make_async_copy(c_ref, c_buf, load_sem.at[1]),
        pltpu.make_async_copy(d_ref.at[1], d_buf.at[1], load_sem.at[2]),
    ]
    for p in range(2):
        loads.append(pltpu.make_async_copy(f_ref.at[:, p], f_buf.at[p], load_sem.at[3 + p]))
    heads = [
        pltpu.make_async_copy(h_ref.at[:, comp, p], h_buf.at[p, comp * 8:(comp + 1) * 8], h_sem.at[p, comp])
        for p in range(2) for comp in range(3)
    ]
    for load in heads + loads:
        load.start()

    barrier = pltpu.get_barrier_semaphore()
    friends = [(row, (col + o) % NC) for o in range(1, NC)]
    friends += [(place(z, (y + dy) % NY), col) for dy in range(1, NY)]
    for dev in friends:
        pl.semaphore_signal(barrier, inc=1, device_id=dev, device_id_type=MESH)
    for dz in (2, 4, 6, 1, 3, 5, 7):
        @pl.when(source if dz % 2 == 0 else other)
        def _():
            there = (place((z + dz) % NZ, y), col)
            pl.semaphore_signal(barrier, inc=1, device_id=there, device_id_type=MESH)

    def partial(stage, value, matrix):
        hi, lo = split(value)
        both = jnp.concatenate([hi, lo], axis=0)
        for b in range(NC):
            m_hi, m_lo = split(matrix[b * W:(b + 1) * W, :])
            one = lax.dot_general(both, m_hi, NT, preferred_element_type=F32)
            two = lax.dot_general(hi, m_lo, NT, preferred_element_type=F32)
            part[stage, b] = one[:V] + (one[V:] + two)

    def exchange(stage, o):
        to = (col + o) % NC
        return remote(part.at[stage, to], got.at[stage, o], a_ss.at[stage, o], a_rs.at[stage, o], (row, to))

    for load in heads:
        load.wait()
    loads[0].wait()
    partial(0, h_buf[0], d_buf.at[0])
    pl.semaphore_wait(barrier, len(friends) + jnp.where(source, NZ - 1, 0))
    for o in range(1, NC):
        @pl.when(col + o < NC)
        def _():
            exchange(0, o).start()
    for p in range(2):
        loads[3 + p].wait()
        f_turn[p, k] = f_buf[p].T
    f_sends = [remote(f_turn.at[p, k], f_turn.at[p, k], fs.at[p], fr.at[p], partner) for p in range(2)]
    for copy in f_sends:
        copy.start()
    loads[1].wait()
    loads[2].wait()
    own[...] = part[0, col]
    for o in range(1, NC):
        @pl.when(col >= o)
        def _():
            exchange(0, o).wait_recv()
            own[...] = own[...] + got[0, o]
    first = own[...]
    sol_ref[0] = first
    partial(1, first, c_buf)
    for o in range(1, NC):
        exchange(1, o).start()

    def give(p):
        return remote(own, S.at[0, 0, y, k], m_ss.at[0], m_rs.at[0], partner)

    def share_z(p, dz):
        slot = SLOT[(NZ - dz) % NZ]
        there = (place((z + dz) % NZ, y), col)
        return remote(S.at[p, 0, y], S.at[p, slot, y], z_ss.at[p, dz], z_rs.at[p, slot], there)

    def wait_z(p, i):
        def wait():
            remote(S.at[p, 0, y], S.at[p, i, y], z_ss.at[p, 1], z_rs.at[p, i], partner).wait_recv()

        if i == 0:
            pl.when(other)(wait)
        else:
            wait()

    def share_y(p, i, dy):
        block = S.at[p, i, y] if p == 1 else S.at[p, :, y]
        there = (place(z, (y + dy) % NY), col)
        return remote(block, block, y_ss.at[p, i, dy], y_rs.at[p, i, dy], there)

    def start_y(p, i):
        for dy in range(1, NY):
            share_y(p, i, dy).start()

    @pl.when(other)
    def _():
        give(0).start()

    @pl.when(source)
    def _():
        S[0, 0, y, k] = first
        remote(own, S.at[0, 0, y, 1 - k], m_ss.at[0], m_rs.at[0], partner).wait_recv()
        for dz in ORDER:
            share_z(0, dz).start()

    def turn(p):
        f_sends[p].wait_recv()
        for kk in range(2):
            hi, lo = split(f_turn[p, kk])
            ft_hi[p, kk * W:(kk + 1) * W, :] = hi
            ft_lo[p, kk * W:(kk + 1) * W, :] = lo

    turn(0)

    moved = part[1, col]
    for o in range(1, NC):
        exchange(1, o).wait_recv()
        moved = moved + got[1, o]
    partial(2, h_buf[1] - moved, d_buf.at[1])

    def deliver(o):
        to = (x + o) % NX
        return remote(part.at[2, pl.ds(to * 2, 2)], pair.at[o, k], b_ss.at[o], b_rs.at[o, k], (row, to * 2 + z % 2))

    def delivered(o, kk):
        return remote(part.at[2, pl.ds(x * 2, 2)], pair.at[o, kk], b_ss.at[o], b_rs.at[o, kk], partner)

    for o in range(1, NX):
        @pl.when(x + o < NX)
        def _():
            deliver(o).start()

    @pl.when(other)
    def _():
        deliver(0).start()

    for i in range(NP):
        wait_z(0, i)
    start_y(0, 0)
    turn(1)

    def reply():
        return remote(S.at[1, 0, y, 1 - k], sol_in, m_ss.at[1], m_rs.at[1], partner)

    @pl.when(source)
    def _():
        S[1, 0, y] = part[2, pl.ds(x * 2, 2)]
        for o in range(1, NX):
            @pl.when(x >= o)
            def _():
                for kk in range(2):
                    delivered(o, kk).wait_recv()
                S[1, 0, y] = S[1, 0, y] + (pair[o, 0] + pair[o, 1])

        delivered(0, 1 - k).wait_recv()
        S[1, 0, y] = S[1, 0, y] + pair[0, 1 - k]
        start_y(1, 0)
        for dz in ORDER:
            share_z(1, dz).start()
        reply().start()
        sol_ref[1] = S[1, 0, y, k]

    def update(p, i):
        s = jnp.concatenate([S[p, i, :, 0].reshape(4 * V, W), S[p, i, :, 1].reshape(4 * V, W)], axis=1)
        hi, lo = split(s)
        both = jnp.concatenate([hi, lo], axis=0)
        parts = []
        for half in range(2):
            at = slice(half * HALF, (half + 1) * HALF)
            one = jnp.dot(both, ft_hi[p, :, at], preferred_element_type=F32)
            two = jnp.dot(hi, ft_lo[p, :, at], preferred_element_type=F32)
            parts.append(one[:4 * V] + (one[4 * V:] + two))
        return parts

    right, left = (x + 1) % NX, (x + NX - 1) % NX

    def target(i):
        return (z + jnp.where(source, EVEN[i], ODD[i])) % NZ // 2

    def piece(n):
        return pl.ds(n * ROWS, ROWS)

    def over(i, half, n):
        to = (left if half else right) * 2 + k
        return remote(acc.at[i, half, piece(n)], M.at[half, piece(n)],
                      o_ss.at[0, half, n], o_rs.at[0, half, n], (row, to))

    def direct(i, half):
        to = (right if half else left) * 2 + k
        return remote(acc.at[i, half], R.at[0, half], e_ss.at[half], e_rs.at[half], (row, to))

    def merged(i, half, n):
        to = (left if half else right) * 2 + k
        return remote(acc.at[i, half, piece(n)], R.at[1, half, piece(n)],
                      o_ss.at[1, half, n], o_rs.at[1, half, n], (row, to))

    def finish(i):
        for dy in range(1, NY):
            share_y(1, i, dy).wait_recv()
        for half, value in enumerate(update(1, i)):
            acc[i, half] = acc[i, half] + value
        to = target(i)

        @pl.when((to - x + NX) % NX == 2)
        def _():
            for n in range(PIECES):
                over(i, 0, n).start()
                over(i, 1, n).start()

        @pl.when(to == right)
        def _():
            direct(i, 1).start()

        @pl.when(to == left)
        def _():
            direct(i, 0).start()

    def merge(i):
        to = target(i)
        for half in range(2):
            @pl.when(to == (left if half else right))
            def _():
                for n in range(PIECES):
                    over(i, half, n).wait_recv()
                    acc[i, half, piece(n)] = acc[i, half, piece(n)] + M[half, piece(n)]
                    merged(i, half, n).start()

    def forward(i):
        wait_z(1, i)
        if i == 0:
            @pl.when(other)
            def _():
                start_y(1, 0)
        else:
            start_y(1, i)

    def begin(i):
        for half, value in enumerate(update(0, i)):
            acc[i, half] = value

    for i in range(NP):
        forward(i)
    for dy in range(1, NY):
        share_y(0, 0, dy).wait_recv()
    for i in range(NP):
        begin(i)
    for i in range(NP):
        finish(i)
        if i >= LAG:
            merge(i - LAG)
    for i in range(NP - LAG, NP):
        merge(i)

    mine = sum(jnp.where(target(i) == x, i, 0) for i in range(NP))
    for half in range(2):
        direct(0, half).wait_recv()
    for n in range(PIECES):
        for half in range(2):
            merged(0, half, n).wait_recv()
            for unit in range(n * ROWS // 8, (n + 1) * ROWS // 8):
                yy, comp = unit // 3, unit % 3
                rows = slice(unit * 8, unit * 8 + 8)
                value = acc[mine, half, rows] + (R[0, half, rows] + R[1, half, rows])
                upd_ref[comp, yy * 8:(yy + 1) * 8, half * HALF:(half + 1) * HALF] = value

    @pl.when(other)
    def _():
        reply().wait_recv()
        sol_ref[1] = sol_in[...]

    for o in range(1, NC):
        @pl.when(col + o < NC)
        def _():
            exchange(0, o).wait_send()

        exchange(1, o).wait_send()
    for o in range(1, NX):
        @pl.when(x + o < NX)
        def _():
            deliver(o).wait_send()

    @pl.when(other)
    def _():
        deliver(0).wait_send()
        give(0).wait_send()

    @pl.when(source)
    def _():
        reply().wait_send()
        for p in range(2):
            for dz in ORDER:
                share_z(p, dz).wait_send()

    for dy in range(1, NY):
        share_y(0, 0, dy).wait_send()
        for i in range(NP):
            share_y(1, i, dy).wait_send()
    for copy in f_sends:
        copy.wait_send()
    for half in range(2):
        direct(0, half).wait_send()
        for n in range(PIECES):
            over(0, half, n).wait_send()
            merged(0, half, n).wait_send()


def body(head_deflections, diag_inverse, coupling, panel_factor, trailing):
    rows = panel_factor.shape[0]
    any_spec = pl.BlockSpec(memory_space=pl.ANY)
    vmem = pl.BlockSpec(memory_space=pltpu.VMEM)
    dma = pltpu.SemaphoreType.DMA
    solved, moved = pl.pallas_call(
        kernel,
        out_shape=(
            jax.ShapeDtypeStruct((2, V, W), F32),
            jax.ShapeDtypeStruct((3, 4 * 8, rows), F32),
        ),
        in_specs=[any_spec] * 4,
        out_specs=(vmem, vmem),
        scratch_shapes=[
            pltpu.VMEM((2, V, W), F32),
            pltpu.VMEM((2, 1024, W), F32),
            pltpu.VMEM((1024, W), F32),
            pltpu.VMEM((2, rows, W), F32),
            pltpu.VMEM((2, 2, W, rows), F32),
            pltpu.VMEM((2, 2 * W, rows), BF16),
            pltpu.VMEM((2, 2 * W, rows), BF16),
            pltpu.VMEM((3, NC, V, W), F32),
            pltpu.VMEM((2, NC, V, W), F32),
            pltpu.VMEM((NX, 2, 2, V, W), F32),
            pltpu.VMEM((V, W), F32),
            pltpu.VMEM((V, W), F32),
            pltpu.VMEM((2, NP, NY, 2, V, W), F32),
            pltpu.VMEM((NP, 2, 4 * V, HALF), F32),
            pltpu.VMEM((2, 4 * V, HALF), F32),
            pltpu.VMEM((2, 2, 4 * V, HALF), F32),
            dma((2, 3)), dma((5,)), dma((2,)), dma((2,)),
            dma((2, NC)), dma((2, NC)),
            dma((NX,)), dma((NX, 2)),
            dma((2,)), dma((2,)),
            dma((2, NZ)), dma((2, NP)),
            dma((2, NP, NY)), dma((2, NP, NY)),
            dma((2,)), dma((2,)),
            dma((2, 2, PIECES)), dma((2, 2, PIECES)),
        ],
        compiler_params=pltpu.CompilerParams(
            collective_id=0, has_side_effects=True, vmem_limit_bytes=int(53.5 * (1 << 20))),
    )(head_deflections, diag_inverse, coupling, panel_factor)
    rest = trailing - jnp.transpose(moved, (1, 0, 2))
    out = jnp.transpose(solved.reshape(2, 3, 8, W), (2, 1, 0, 3))
    return (out, rest)


def solution(mesh):
    placed = (
        P("row", None, None, "col"),
        P(None, None, "col"),
        P(None, "col"),
        P("row", None, "col"),
        P("col", None, "row"),
    )
    return jax.shard_map(
        body,
        mesh=mesh,
        in_specs=placed,
        out_specs=(P("row", None, None, "col"), P("col", None, "row")),
        check_vma=False,
    )
```

```python
import functools

import jax
import jax.numpy as jnp
from jax import lax
from jax.experimental import pallas as pl
from jax.experimental.pallas import tpu as pltpu
from jax.sharding import PartitionSpec as P

MESH = pl.DeviceIdType.MESH
F32 = jnp.float32
BF16 = jnp.bfloat16
NX, NY, NZ = 4, 4, 8
NC = 8
V = 24
W = 128
HALF = 512
LAG = 3
PIECES = 3
ROWS = 4 * V // PIECES
ORDER = (1, 7, 2, 6, 3, 5, 4)
SLOT = {0: 0, 6: 1, 2: 2, 4: 3, 7: 0, 1: 1, 5: 2, 3: 3}
EVEN = (0, 6, 2, 4)
ODD = (7, 1, 5, 3)
NP = 4
NT = (((1,), (1,)), ((), ()))


def split(value):
    high = value.astype(BF16)
    return high, (value - high.astype(F32)).astype(BF16)


def kernel(h_ref, d_ref, c_ref, f_ref, sol_ref, upd_ref,
           h_buf, d_buf, c_buf, f_buf, f_turn, ft_hi, ft_lo, part, got, pair, own, sol_in, S, acc, M, R,
           h_sem, load_sem, fs, fr, a_ss, a_rs, b_ss, b_rs, m_ss, m_rs, z_ss, z_rs, y_ss, y_rs, e_ss, e_rs, o_ss, o_rs):
    row, col = lax.axis_index("row"), lax.axis_index("col")
    z, y = row // NY, row % NY
    x, k = col // 2, col % 2
    source = z % 2 == k
    other = z % 2 != k
    partner = (row, x * 2 + 1 - k)

    def place(zz, yy):
        return zz * NY + yy

    def remote(src, dst, ss, rs, to):
        return pltpu.make_async_remote_copy(
            src_ref=src, dst_ref=dst, send_sem=ss, recv_sem=rs, device_id=to, device_id_type=MESH)

    loads = [
        pltpu.make_async_copy(d_ref.at[0], d_buf.at[0], load_sem.at[0]),
        pltpu.make_async_copy(c_ref, c_buf, load_sem.at[1]),
        pltpu.make_async_copy(d_ref.at[1], d_buf.at[1], load_sem.at[2]),
    ]
    for p in range(2):
        loads.append(pltpu.make_async_copy(f_ref.at[:, p], f_buf.at[p], load_sem.at[3 + p]))
    heads = [
        pltpu.make_async_copy(h_ref.at[:, comp, p], h_buf.at[p, comp * 8:(comp + 1) * 8], h_sem.at[p, comp])
        for p in range(2) for comp in range(3)
    ]
    for load in heads + loads:
        load.start()

    barrier = pltpu.get_barrier_semaphore()
    friends = [(row, (col + o) % NC) for o in range(1, NC)]
    friends += [(place(z, (y + dy) % NY), col) for dy in range(1, NY)]
    for dev in friends:
        pl.semaphore_signal(barrier, inc=1, device_id=dev, device_id_type=MESH)
    for dz in (2, 4, 6, 1, 3, 5, 7):
        @pl.when(source if dz % 2 == 0 else other)
        def _():
            there = (place((z + dz) % NZ, y), col)
            pl.semaphore_signal(barrier, inc=1, device_id=there, device_id_type=MESH)

    def partial(stage, value, matrix):
        hi, lo = split(value)
        both = jnp.concatenate([hi, lo], axis=0)
        for b in range(NC):
            m_hi, m_lo = split(matrix[b * W:(b + 1) * W, :])
            one = lax.dot_general(both, m_hi, NT, preferred_element_type=F32)
            two = lax.dot_general(hi, m_lo, NT, preferred_element_type=F32)
            part[stage, b] = one[:V] + (one[V:] + two)

    def exchange(stage, o):
        to = (col + o) % NC
        return remote(part.at[stage, to], got.at[stage, o], a_ss.at[stage, o], a_rs.at[stage, o], (row, to))

    for load in heads:
        load.wait()
    loads[0].wait()
    partial(0, h_buf[0], d_buf.at[0])
    pl.semaphore_wait(barrier, len(friends) + jnp.where(source, NZ - 1, 0))
    for o in range(1, NC):
        @pl.when(col + o < NC)
        def _():
            exchange(0, o).start()
    for p in range(2):
        loads[3 + p].wait()
        f_turn[p, k] = f_buf[p].T
    f_sends = [remote(f_turn.at[p, k], f_turn.at[p, k], fs.at[p], fr.at[p], partner) for p in range(2)]
    for copy in f_sends:
        copy.start()
    loads[1].wait()
    loads[2].wait()
    own[...] = part[0, col]
    for o in range(1, NC):
        @pl.when(col >= o)
        def _():
            exchange(0, o).wait_recv()
            own[...] = own[...] + got[0, o]
    first = own[...]
    sol_ref[0] = first
    partial(1, first, c_buf)
    for o in range(1, NC):
        exchange(1, o).start()

    def give(p):
        return remote(own, S.at[0, 0, y, k], m_ss.at[0], m_rs.at[0], partner)

    def share_z(p, dz):
        slot = SLOT[(NZ - dz) % NZ]
        there = (place((z + dz) % NZ, y), col)
        return remote(S.at[p, 0, y], S.at[p, slot, y], z_ss.at[p, dz], z_rs.at[p, slot], there)

    def wait_z(p, i):
        def wait():
            remote(S.at[p, 0, y], S.at[p, i, y], z_ss.at[p, 1], z_rs.at[p, i], partner).wait_recv()

        if i == 0:
            pl.when(other)(wait)
        else:
            wait()

    def share_y(p, i, dy):
        block = S.at[p, i, y] if p == 1 else S.at[p, :, y]
        there = (place(z, (y + dy) % NY), col)
        return remote(block, block, y_ss.at[p, i, dy], y_rs.at[p, i, dy], there)

    def start_y(p, i):
        for dy in range(1, NY):
            share_y(p, i, dy).start()

    @pl.when(other)
    def _():
        give(0).start()

    @pl.when(source)
    def _():
        S[0, 0, y, k] = first
        remote(own, S.at[0, 0, y, 1 - k], m_ss.at[0], m_rs.at[0], partner).wait_recv()
        for dz in ORDER:
            share_z(0, dz).start()

    def turn(p):
        f_sends[p].wait_recv()
        for kk in range(2):
            hi, lo = split(f_turn[p, kk])
            ft_hi[p, kk * W:(kk + 1) * W, :] = hi
            ft_lo[p, kk * W:(kk + 1) * W, :] = lo

    turn(0)

    moved = part[1, col]
    for o in range(1, NC):
        exchange(1, o).wait_recv()
        moved = moved + got[1, o]
    partial(2, h_buf[1] - moved, d_buf.at[1])

    def deliver(o):
        to = (x + o) % NX
        return remote(part.at[2, pl.ds(to * 2, 2)], pair.at[o, k], b_ss.at[o], b_rs.at[o, k], (row, to * 2 + z % 2))

    def delivered(o, kk):
        return remote(part.at[2, pl.ds(x * 2, 2)], pair.at[o, kk], b_ss.at[o], b_rs.at[o, kk], partner)

    for o in range(1, NX):
        @pl.when(x + o < NX)
        def _():
            deliver(o).start()

    @pl.when(other)
    def _():
        deliver(0).start()

    for i in range(NP):
        wait_z(0, i)
    start_y(0, 0)
    turn(1)

    def reply():
        return remote(S.at[1, 0, y, 1 - k], sol_in, m_ss.at[1], m_rs.at[1], partner)

    @pl.when(source)
    def _():
        S[1, 0, y] = part[2, pl.ds(x * 2, 2)]
        for o in range(1, NX):
            @pl.when(x >= o)
            def _():
                for kk in range(2):
                    delivered(o, kk).wait_recv()
                S[1, 0, y] = S[1, 0, y] + (pair[o, 0] + pair[o, 1])

        delivered(0, 1 - k).wait_recv()
        S[1, 0, y] = S[1, 0, y] + pair[0, 1 - k]
        start_y(1, 0)
        for dz in ORDER:
            share_z(1, dz).start()
        reply().start()
        sol_ref[1] = S[1, 0, y, k]

    def update(p, i):
        s = jnp.concatenate([S[p, i, :, 0].reshape(4 * V, W), S[p, i, :, 1].reshape(4 * V, W)], axis=1)
        hi, lo = split(s)
        both = jnp.concatenate([hi, lo], axis=0)
        parts = []
        for half in range(2):
            at = slice(half * HALF, (half + 1) * HALF)
            one = jnp.dot(both, ft_hi[p, :, at], preferred_element_type=F32)
            two = jnp.dot(hi, ft_lo[p, :, at], preferred_element_type=F32)
            parts.append(one[:4 * V] + (one[4 * V:] + two))
        return parts

    right, left = (x + 1) % NX, (x + NX - 1) % NX

    def target(i):
        return (z + jnp.where(source, EVEN[i], ODD[i])) % NZ // 2

    def piece(n):
        return pl.ds(n * ROWS, ROWS)

    def over(i, half, n):
        to = (left if half else right) * 2 + k
        return remote(acc.at[i, half, piece(n)], M.at[half, piece(n)],
                      o_ss.at[0, half, n], o_rs.at[0, half, n], (row, to))

    def direct(i, half):
        to = (right if half else left) * 2 + k
        return remote(acc.at[i, half], R.at[0, half], e_ss.at[half], e_rs.at[half], (row, to))

    def merged(i, half, n):
        to = (left if half else right) * 2 + k
        return remote(acc.at[i, half, piece(n)], R.at[1, half, piece(n)],
                      o_ss.at[1, half, n], o_rs.at[1, half, n], (row, to))

    def finish(i):
        for dy in range(1, NY):
            share_y(1, i, dy).wait_recv()
        for half, value in enumerate(update(1, i)):
            acc[i, half] = acc[i, half] + value
        to = target(i)

        @pl.when((to - x + NX) % NX == 2)
        def _():
            for n in range(PIECES):
                over(i, 0, n).start()
                over(i, 1, n).start()

        @pl.when(to == right)
        def _():
            direct(i, 1).start()

        @pl.when(to == left)
        def _():
            direct(i, 0).start()

    def merge(i):
        to = target(i)
        for half in range(2):
            @pl.when(to == (left if half else right))
            def _():
                for n in range(PIECES):
                    over(i, half, n).wait_recv()
                    acc[i, half, piece(n)] = acc[i, half, piece(n)] + M[half, piece(n)]
                    merged(i, half, n).start()

    def forward(i):
        wait_z(1, i)
        if i == 0:
            @pl.when(other)
            def _():
                start_y(1, 0)
        else:
            start_y(1, i)

    def begin(i):
        for half, value in enumerate(update(0, i)):
            acc[i, half] = value

    for i in range(NP):
        forward(i)
    for dy in range(1, NY):
        share_y(0, 0, dy).wait_recv()
    for i in range(NP):
        begin(i)
    for i in range(NP):
        finish(i)
        if i >= LAG:
            merge(i - LAG)
    for i in range(NP - LAG, NP):
        merge(i)

    mine = sum(jnp.where(target(i) == x, i, 0) for i in range(NP))
    for half in range(2):
        direct(0, half).wait_recv()
    for n in range(PIECES):
        for half in range(2):
            merged(0, half, n).wait_recv()
            for unit in range(n * ROWS // 8, (n + 1) * ROWS // 8):
                yy, comp = unit // 3, unit % 3
                rows = slice(unit * 8, unit * 8 + 8)
                value = acc[mine, half, rows] + (R[0, half, rows] + R[1, half, rows])
                upd_ref[comp, yy * 8:(yy + 1) * 8, half * HALF:(half + 1) * HALF] = value

    @pl.when(other)
    def _():
        reply().wait_recv()
        sol_ref[1] = sol_in[...]

    for o in range(1, NC):
        @pl.when(col + o < NC)
        def _():
            exchange(0, o).wait_send()

        exchange(1, o).wait_send()
    for o in range(1, NX):
        @pl.when(x + o < NX)
        def _():
            deliver(o).wait_send()

    @pl.when(other)
    def _():
        deliver(0).wait_send()
        give(0).wait_send()

    @pl.when(source)
    def _():
        reply().wait_send()
        for p in range(2):
            for dz in ORDER:
                share_z(p, dz).wait_send()

    for dy in range(1, NY):
        share_y(0, 0, dy).wait_send()
        for i in range(NP):
            share_y(1, i, dy).wait_send()
    for copy in f_sends:
        copy.wait_send()
    for half in range(2):
        direct(0, half).wait_send()
        for n in range(PIECES):
            over(0, half, n).wait_send()
            merged(0, half, n).wait_send()


def body(head_deflections, diag_inverse, coupling, panel_factor, trailing):
    rows = panel_factor.shape[0]
    any_spec = pl.BlockSpec(memory_space=pl.ANY)
    vmem = pl.BlockSpec(memory_space=pltpu.VMEM)
    dma = pltpu.SemaphoreType.DMA
    solved, moved = pl.pallas_call(
        kernel,
        out_shape=(
            jax.ShapeDtypeStruct((2, V, W), F32),
            jax.ShapeDtypeStruct((3, 4 * 8, rows), F32),
        ),
        in_specs=[any_spec] * 4,
        out_specs=(vmem, vmem),
        scratch_shapes=[
            pltpu.VMEM((2, V, W), F32),
            pltpu.VMEM((2, 1024, W), F32),
            pltpu.VMEM((1024, W), F32),
            pltpu.VMEM((2, rows, W), F32),
            pltpu.VMEM((2, 2, W, rows), F32),
            pltpu.VMEM((2, 2 * W, rows), BF16),
            pltpu.VMEM((2, 2 * W, rows), BF16),
            pltpu.VMEM((3, NC, V, W), F32),
            pltpu.VMEM((2, NC, V, W), F32),
            pltpu.VMEM((NX, 2, 2, V, W), F32),
            pltpu.VMEM((V, W), F32),
            pltpu.VMEM((V, W), F32),
            pltpu.VMEM((2, NP, NY, 2, V, W), F32),
            pltpu.VMEM((NP, 2, 4 * V, HALF), F32),
            pltpu.VMEM((2, 4 * V, HALF), F32),
            pltpu.VMEM((2, 2, 4 * V, HALF), F32),
            dma((2, 3)), dma((5,)), dma((2,)), dma((2,)),
            dma((2, NC)), dma((2, NC)),
            dma((NX,)), dma((NX, 2)),
            dma((2,)), dma((2,)),
            dma((2, NZ)), dma((2, NP)),
            dma((2, NP, NY)), dma((2, NP, NY)),
            dma((2,)), dma((2,)),
            dma((2, 2, PIECES)), dma((2, 2, PIECES)),
        ],
        compiler_params=pltpu.CompilerParams(
            collective_id=0, has_side_effects=True, vmem_limit_bytes=int(53.5 * (1 << 20))),
    )(head_deflections, diag_inverse, coupling, panel_factor)
    rest = trailing - jnp.transpose(moved, (1, 0, 2))
    out = jnp.transpose(solved.reshape(2, 3, 8, W), (2, 1, 0, 3))
    return (out, rest)


def solution(mesh):
    placed = (
        P("row", None, None, "col"),
        P(None, None, "col"),
        P(None, "col"),
        P("row", None, "col"),
        P("col", None, "row"),
    )
    return jax.shard_map(
        body,
        mesh=mesh,
        in_specs=placed,
        out_specs=(P("row", None, None, "col"), P("col", None, "row")),
        check_vma=False,
    )
```
